32 devices in a mesh: dp: 16 (over z, y, x), shard: 2 (over core).
Axes of the slice: x: 2, y: 2, z: 4, core: 2. Of those that a mesh axis runs over, the one named last changes fastest.
Arguments:
- tokens: bfloat16 [16384, 1024], P(('dp', 'shard')), may hold values from -6 to 6
- cotangent: bfloat16 [16384, 1024], P(('dp', 'shard')), may hold values from -6 to 6
- lengths: int32 [32], P(('dp', 'shard')), may hold values from 1 to 512, as said below
- w_in: float32 [1024, 10240], P('shard'), may hold values from -0.1875 to 0.1875
- w_out: float32 [5120, 1024], P('shard')
- gains: float32 [2304], P('shard'), may hold values from 0.5 to 1.5
- first_in: float32 [1024, 10240], P('shard'), may hold values from -48 to 48
- first_out: float32 [5120, 1024], P('shard'), may hold values from -48 to 48
- gain_first: float32 [2304], P('shard'), may hold values from -96 to 96
- second_in: float32 [1024, 10240], P('shard'), may hold values from 212.992 to 868.352
- second_out: float32 [5120, 1024], P('shard'), may hold values from 212.992 to 868.352
- gain_second: float32 [2304], P('shard'), may hold values from 851.968 to 3440.64
Outputs:
- layer_output: bfloat16 [16384, 1024], P(('dp', 'shard'))
- layer_input_gradient: bfloat16 [16384, 1024], P(('dp', 'shard'))
- new_w_in: float32 [1024, 10240], P('shard')
- new_w_out: float32 [5120, 1024], P('shard')
- new_gains: float32 [2304], P('shard')
- new_first_in: float32 [1024, 10240], P('shard')
- new_first_out: float32 [5120, 1024], P('shard')
- new_gain_first: float32 [2304], P('shard')
- new_second_in: float32 [1024, 10240], P('shard')
- new_second_out: float32 [5120, 1024], P('shard')
- new_gain_second: float32 [2304], P('shard')
- valid_rms: float32 [2], replicated
The draws below stay inside these ranges and needn't reach their ends.
Inputs may be any that keep to these rules, and one draw needn't show every extreme that they name: `lengths`: valid tokens of each slot, counted from its first row; in every draw one slot holds exactly 512.
All inputs are finite; a program needn't handle non-finite values.
Results may differ from the reference program's by a relative error of at most 0.013.
The reference program's roundings to bfloat16 on the way count: a program that leaves them out, or rounds other values in their place, can miss the bound.
Values may be sent and summed in bfloat16 or wider, within the bound.
No kernel may reach another device: no remote copies, remote signals or barrier semaphores. Data moves between devices by JAX's collectives and lax.ppermute only.
A program may use at most 448 MiB of HBM per device.

```python
import math
import jax
import jax.numpy as jnp
from jax import lax

MODEL_WIDTH = 1024
FF = 3072
QUERY_HEADS = 16
KEY_VALUE_HEADS = 8
HEAD_SIZE = 128
SLOT_ROWS = 512
STEP = 7
QKVC = 4096
INC = 10240
OUTR = 5120
GN = 2304
SLOT_TOTAL = 32
TOKENS = 16384


def draw_lengths(key, part):
    key = jax.random.fold_in(key, 11)
    number_of_slots = SLOT_TOTAL
    slot_index = jnp.arange(number_of_slots, dtype=jnp.int32)
    floor_length = SLOT_ROWS // 3
    ramp = floor_length + (SLOT_ROWS - floor_length) * slot_index // max(number_of_slots - 1, 1)
    jitter = jax.random.randint(jax.random.fold_in(key, 1), (number_of_slots,), -(SLOT_ROWS // 8), SLOT_ROWS // 8 + 1)
    chosen = jax.random.randint(jax.random.fold_in(key, 2), (), 0, number_of_slots)
    values = jnp.clip(ramp + jitter, 1, SLOT_ROWS)
    return jnp.where(slot_index == chosen, SLOT_ROWS, values).astype(jnp.int32)


def draw_w_out(key, part):
    key = jax.random.fold_in(key, 23)
    row_index = jnp.arange(OUTR)
    attn_scale = (SLOT_ROWS / 16.0) ** 0.5 / (QUERY_HEADS * HEAD_SIZE) ** 0.5
    down_scale = FF ** (-0.5)
    row_scale = jnp.where(row_index < QUERY_HEADS * HEAD_SIZE, attn_scale, down_scale).astype(jnp.float32)[:, None]
    base = jax.random.normal(key, (OUTR, MODEL_WIDTH), jnp.float32)
    return base * row_scale


def block_levels(key, shape, pieces, least, largest):
    def one(dim, blocks):
        heights = jax.random.uniform(jax.random.fold_in(jax.random.fold_in(key, 6), dim), (blocks,), jnp.float32, least / len(pieces), largest / len(pieces))
        return jnp.repeat(jnp.exp(heights), shape[dim] // blocks).reshape((-1,) + (1,) * (len(shape) - dim - 1))

    loudness = one(*pieces[0])
    for cut in pieces[1:]:
        loudness = loudness * one(*cut)
    return loudness


def gaussian(rng, extent, deviation, bound, split=(), kind=jnp.bfloat16):
    entries = jax.random.normal(rng, extent, jnp.float32) * deviation
    if len(split) > 0:
        entries = block_levels(rng, extent, split, -0.22, 0.18) * entries
    return jnp.clip(entries, min=-bound, max=bound).astype(kind)


def setup_inputs(seed: int = 0) -> dict:
    keys = jax.random.split(jax.random.key(seed), 13)
    return {
        "tokens": gaussian(keys[0], (TOKENS, MODEL_WIDTH), 1.0, 6.0, ((0, 32),)),
        "cotangent": gaussian(keys[1], (TOKENS, MODEL_WIDTH), 1.0, 6.0, ((0, 32),)),
        "lengths": draw_lengths(jax.random.fold_in(keys[12], 71), 0),
        "w_in": gaussian(keys[3], (MODEL_WIDTH, INC), MODEL_WIDTH ** -0.5, 0.1875, ((0, 2),), jnp.float32),
        "w_out": draw_w_out(jax.random.fold_in(keys[12], 71), 0),
        "gains": jnp.clip(1.0 + 0.1 * jax.random.normal(keys[5], (GN,), jnp.float32), 0.5, 1.5),
        "first_in": gaussian(keys[6], (MODEL_WIDTH, INC), (0.06 * TOKENS ** 0.5), 48.0, ((0, 2),), jnp.float32),
        "first_out": gaussian(keys[7], (OUTR, MODEL_WIDTH), (0.06 * TOKENS ** 0.5), 48.0, ((0, 2),), jnp.float32),
        "gain_first": gaussian(keys[8], (GN,), (0.12 * TOKENS ** 0.5), 96.0, ((0, 2),), jnp.float32),
        "second_in": jnp.clip(jnp.exp(math.log(868.352) - 1.40534252 * jax.random.uniform(keys[9], (MODEL_WIDTH, INC), jnp.float32) ** block_levels(keys[9], (MODEL_WIDTH, INC), ((0, 2),), -0.2, 0.2)), 212.992, 868.352),
        "second_out": jnp.clip(jnp.exp(math.log(868.352) - 1.40534252 * jax.random.uniform(keys[10], (OUTR, MODEL_WIDTH), jnp.float32) ** block_levels(keys[10], (OUTR, MODEL_WIDTH), ((0, 2),), -0.2, 0.2)), 212.992, 868.352),
        "gain_second": jnp.clip(jnp.exp(math.log(3440.64) - 1.3958638 * jax.random.uniform(keys[11], (GN,), jnp.float32) ** block_levels(keys[11], (GN,), ((0, 2),), -0.2, 0.2)), 851.968, 3440.64),
    }


EPSILON = 1e-06
BETA_ONE = 0.9
BETA_TWO = 0.95
ADAM_EPSILON = 1e-08
MATRIX_RATE = 0.05
GAIN_RATE = 0.3
MATRIX_DECAY = 0.1
NEG_LARGE = -1e+30

@jax.custom_vjp
def low(v):
    return lax.optimization_barrier(v.astype(jnp.bfloat16)).astype(jnp.float32)

@jax.custom_vjp
def low_back(v):
    return v

def low_keep(v):
    return (low(v), None)

def low_pass(kept, grad):
    return (grad,)

def back_keep(v):
    return (v, None)

def back_low(kept, grad):
    return (low(grad),)
low.defvjp(low_keep, low_pass)
low_back.defvjp(back_keep, back_low)

def rms_scale(values, gain):
    return values * lax.rsqrt(lax.optimization_barrier(jnp.mean(values * values, axis=-1, keepdims=True)) + EPSILON) * gain

def rope_tables(length, size):
    positions = jnp.arange(length, dtype=jnp.float32)
    half_index = jnp.arange(size // 2, dtype=jnp.float32)
    frequency = jnp.exp(half_index * (-2.0 * math.log(1000000.0) / size))
    angles = positions[:, None] * frequency[None, :]
    angles = jnp.concatenate([angles, angles], axis=1)
    return (jnp.cos(angles), jnp.sin(angles))

def rotate(values, cosine, sine):
    half_size = values.shape[-1] // 2
    turned = jnp.concatenate([-values[..., half_size:], values[..., :half_size]], axis=-1)
    return values * cosine[:, None, :] + turned * sine[:, None, :]

def prepare(unnormed_rows, gain_q, gain_k, cosine, sine):
    leading_rows = unnormed_rows.shape[:-1]
    queries = unnormed_rows[..., :QUERY_HEADS * HEAD_SIZE].reshape(leading_rows + (QUERY_HEADS, HEAD_SIZE))
    key_head_rows = unnormed_rows[..., QUERY_HEADS * HEAD_SIZE:(QUERY_HEADS + KEY_VALUE_HEADS) * HEAD_SIZE].reshape(leading_rows + (KEY_VALUE_HEADS, HEAD_SIZE))
    value_head_rows = unnormed_rows[..., (QUERY_HEADS + KEY_VALUE_HEADS) * HEAD_SIZE:].reshape(leading_rows + (KEY_VALUE_HEADS, HEAD_SIZE))
    queries = rotate(rms_scale(queries, gain_q), cosine, sine)
    key_head_rows = rotate(rms_scale(key_head_rows, gain_k), cosine, sine)
    return (queries, key_head_rows, value_head_rows)

def gated_unit(mixed):
    return jax.nn.silu(mixed[..., :FF]) * mixed[..., FF:]

def adamw_update(weight, first, second, gradient, rate, decay):
    first = BETA_ONE * first + (1.0 - BETA_ONE) * gradient
    second = BETA_TWO * second + (1.0 - BETA_TWO) * gradient * gradient
    corr_one = 1.0 - BETA_ONE ** STEP
    corr_two = 1.0 - BETA_TWO ** STEP
    update = first / corr_one / (jnp.sqrt(second / corr_two) + ADAM_EPSILON) + decay * weight
    return (weight - rate * update, first, second)

def slot_forward(params, slot_tokens, length):
    weight_in, weight_out, gain_all = params
    highest = lax.Precision.HIGHEST
    cosine, sine = rope_tables(SLOT_ROWS, HEAD_SIZE)
    gain_in = gain_all[:MODEL_WIDTH]
    gain_post = gain_all[MODEL_WIDTH:2 * MODEL_WIDTH]
    gain_query = gain_all[2 * MODEL_WIDTH:2 * MODEL_WIDTH + HEAD_SIZE]
    gain_key = gain_all[2 * MODEL_WIDTH + HEAD_SIZE:]
    normed = low(rms_scale(slot_tokens, gain_in))
    unnormed_rows = low_back(jnp.dot(normed, weight_in[:, :QKVC], precision=highest))
    queries, key_head_rows, value_head_rows = prepare(unnormed_rows, gain_query, gain_key, cosine, sine)
    queries = low(queries)
    key_head_rows = low(key_head_rows)
    value_head_rows = low(value_head_rows)
    query_group_width = QUERY_HEADS // KEY_VALUE_HEADS
    key_head_rows = jnp.repeat(key_head_rows, query_group_width, axis=1)
    value_head_rows = jnp.repeat(value_head_rows, query_group_width, axis=1)
    scores = low_back(jnp.einsum('qhd,khd->hqk', queries, key_head_rows, precision=highest) * HEAD_SIZE ** (-0.5))
    row_index = jnp.arange(SLOT_ROWS, dtype=jnp.int32)
    allowed = (row_index[None, :] <= row_index[:, None]) & (row_index[None, :] < length)
    scores = jnp.where(allowed[None], scores, NEG_LARGE)
    soft_weights = low(jax.nn.softmax(scores, axis=-1))
    attended = jnp.einsum('hqk,khd->qhd', soft_weights, value_head_rows, precision=highest).reshape(SLOT_ROWS, QUERY_HEADS * HEAD_SIZE)
    attended = low(low_back(attended))
    middle = slot_tokens + low_back(jnp.dot(attended, weight_out[:QUERY_HEADS * HEAD_SIZE], precision=highest))
    normed_post = low(rms_scale(middle, gain_post))
    mixed = low_back(jnp.dot(normed_post, weight_in[:, QKVC:], precision=highest))
    hidden = low(gated_unit(mixed))
    return middle + jnp.dot(hidden, weight_out[QUERY_HEADS * HEAD_SIZE:], precision=highest)

def reference(tokens, cotangent, lengths, w_in, w_out, gains, first_in, first_out, gain_first, second_in, second_out, gain_second):
    params = (w_in.astype(jnp.bfloat16).astype(jnp.float32), w_out.astype(jnp.bfloat16).astype(jnp.float32), gains.astype(jnp.bfloat16).astype(jnp.float32))
    layer_inputs = tokens.astype(jnp.float32).reshape(SLOT_TOTAL, SLOT_ROWS, MODEL_WIDTH)

    def forward(weights, slot_inputs):

        def slot_step(carry_value, slot_item):
            return (carry_value, jax.checkpoint(slot_forward)(weights, slot_item[0], slot_item[1]))
        return lax.scan(slot_step, jnp.zeros((), jnp.float32), (slot_inputs, lengths))[1]
    outputs, backward_function = jax.vjp(forward, params, layer_inputs)
    positions = jnp.arange(SLOT_ROWS, dtype=jnp.int32)
    valid_row_count = (positions[None, :] < lengths[:, None]).astype(jnp.float32)[:, :, None]
    parameter_gradients, input_gradients = backward_function(cotangent.astype(jnp.float32).reshape(SLOT_TOTAL, SLOT_ROWS, MODEL_WIDTH) * valid_row_count)
    layer_output = outputs.reshape(TOKENS, MODEL_WIDTH).astype(jnp.bfloat16)
    layer_input_gradient = input_gradients.reshape(TOKENS, MODEL_WIDTH).astype(jnp.bfloat16)
    output_values = layer_output.astype(jnp.float32).reshape(SLOT_TOTAL, SLOT_ROWS, MODEL_WIDTH)
    value_gradients = layer_input_gradient.astype(jnp.float32).reshape(SLOT_TOTAL, SLOT_ROWS, MODEL_WIDTH)
    number_of_slots = jnp.sum(valid_row_count) * MODEL_WIDTH
    valid_rms = jnp.sqrt(jnp.stack([jnp.sum(valid_row_count * output_values * output_values), jnp.sum(valid_row_count * value_gradients * value_gradients)]) / number_of_slots)
    new_w_in, new_first_in, new_second_in = adamw_update(w_in, first_in, second_in, parameter_gradients[0], MATRIX_RATE, MATRIX_DECAY)
    new_w_out, new_first_out, new_second_out = adamw_update(w_out, first_out, second_out, parameter_gradients[1], MATRIX_RATE, MATRIX_DECAY)
    new_gains, new_gain_first, new_gain_second = adamw_update(gains, gain_first, gain_second, parameter_gradients[2], GAIN_RATE, 0.0)
    return (layer_output, layer_input_gradient, new_w_in, new_w_out, new_gains, new_first_in, new_first_out, new_gain_first, new_second_in, new_second_out, new_gain_second, valid_rms)
```

```python
import math

import jax
import jax.numpy as jnp
import numpy as np
from jax import lax
from jax.experimental import pallas as pl
from jax.experimental.pallas import tpu as pltpu
from jax.sharding import PartitionSpec as P

MODEL_WIDTH = 1024
FF = 3072
QUERY_HEADS = 16
KEY_VALUE_HEADS = 8
HEAD_SIZE = 128
SLOT_ROWS = 512
STEP = 7
QKVC = 4096
GN = 2304


EPSILON = 1e-06
BETA_ONE = 0.9
BETA_TWO = 0.95
ADAM_EPSILON = 1e-08
MATRIX_RATE = 0.05
GAIN_RATE = 0.3
MATRIX_DECAY = 0.1
NEG_LARGE = -1e30


def rms_scale(values, gain):
    return values * lax.rsqrt(jnp.mean(values * values, axis=-1, keepdims=True) + EPSILON) * gain


def rope_tables(length, size):
    positions = jnp.arange(length, dtype=jnp.float32)
    half_index = jnp.arange(size // 2, dtype=jnp.float32)
    frequency = jnp.exp(half_index * (-2.0 * math.log(1000000.0) / size))
    angles = positions[:, None] * frequency[None, :]
    angles = jnp.concatenate([angles, angles], axis=1)
    return (jnp.cos(angles), jnp.sin(angles))


def rotate(values, cosine, sine):
    half_size = values.shape[-1] // 2
    turned = jnp.concatenate([-values[..., half_size:], values[..., :half_size]], axis=-1)
    return values * cosine[:, None, :] + turned * sine[:, None, :]


def prepare(unnormed_rows, gain_q, gain_k, cosine, sine):
    leading_rows = unnormed_rows.shape[:-1]
    queries = unnormed_rows[..., : QUERY_HEADS * HEAD_SIZE].reshape(
        leading_rows + (QUERY_HEADS, HEAD_SIZE)
    )
    key_head_rows = unnormed_rows[
        ..., QUERY_HEADS * HEAD_SIZE : (QUERY_HEADS + KEY_VALUE_HEADS) * HEAD_SIZE
    ].reshape(leading_rows + (KEY_VALUE_HEADS, HEAD_SIZE))
    value_head_rows = unnormed_rows[..., (QUERY_HEADS + KEY_VALUE_HEADS) * HEAD_SIZE :].reshape(
        leading_rows + (KEY_VALUE_HEADS, HEAD_SIZE)
    )
    queries = rotate(rms_scale(queries, gain_q), cosine, sine)
    key_head_rows = rotate(rms_scale(key_head_rows, gain_k), cosine, sine)
    return (queries, key_head_rows, value_head_rows)


def gated_unit(mixed):
    return jax.nn.silu(mixed[..., :FF]) * mixed[..., FF:]


def adamw_update(weight, first, second, gradient, rate, decay):
    first = BETA_ONE * first + (1.0 - BETA_ONE) * gradient
    second = BETA_TWO * second + (1.0 - BETA_TWO) * gradient * gradient
    corr_one = 1.0 - BETA_ONE**STEP
    corr_two = 1.0 - BETA_TWO**STEP
    update = first / corr_one / (jnp.sqrt(second / corr_two) + ADAM_EPSILON) + decay * weight
    return (weight - rate * update, first, second)


def outer_sum(left, right):
    return lax.dot_general(
        left, right, (((0,), (0,)), ((), ())), preferred_element_type=jnp.float32
    )


def back_product(gradient, weight):
    return lax.dot_general(
        gradient, weight, (((1,), (1,)), ((), ())), preferred_element_type=jnp.float32
    )


def key_mask(row_count, key_reach, length):
    query_pos = jnp.arange(row_count, dtype=jnp.int32)
    key_pos = jnp.arange(key_reach, dtype=jnp.int32)
    return (key_pos[None, :] <= query_pos[:, None]) & (key_pos[None, :] < length)


def slot_attention(query_low, key_low, value_low, length):
    block_rows = min(512, SLOT_ROWS)
    score_scale = HEAD_SIZE ** (-0.5)
    scores = (
        jnp.einsum("hgqd,hkd->hgqk", query_low, key_low, preferred_element_type=jnp.float32)
        * score_scale
    )
    scores = jnp.where(key_mask(block_rows, block_rows, length), scores, NEG_LARGE)
    row_peak = jnp.max(scores, axis=-1, keepdims=True)
    exp_values = jnp.exp(scores - row_peak)
    exp_total = jnp.sum(exp_values, axis=-1, keepdims=True)
    soft_weights = (exp_values / exp_total).astype(jnp.bfloat16)
    outputs = [
        jnp.einsum(
            "hgqk,hkd->hgqd", soft_weights, value_low, preferred_element_type=jnp.float32
        ).astype(jnp.bfloat16)
    ]
    totals = [row_peak + jnp.log(exp_total)]
    return (jnp.concatenate(outputs, axis=2), jnp.concatenate(totals, axis=2))


def slot_attention_back(query_low, key_low, value_low, totals, heads_gradient, length):
    block_rows = min(512, SLOT_ROWS)
    score_scale = HEAD_SIZE ** (-0.5)
    grad_keys = jnp.zeros(key_low.shape, jnp.float32)
    value_gradients = jnp.zeros(value_low.shape, jnp.float32)
    scores = (
        jnp.einsum("hgqd,hkd->hgqk", query_low, key_low, preferred_element_type=jnp.float32)
        * score_scale
    )
    allowed = key_mask(block_rows, block_rows, length)
    soft_weights = jnp.where(allowed, jnp.exp(scores - totals[:, :, 0:block_rows]), 0.0)
    back_soft = jnp.einsum(
        "hgqd,hkd->hgqk", heads_gradient, value_low, preferred_element_type=jnp.float32
    )
    inner_sums = jnp.sum(soft_weights * back_soft, axis=-1, keepdims=True)
    back_scores = (soft_weights * (back_soft - inner_sums)).astype(jnp.bfloat16)
    query_parts = [
        jnp.einsum("hgqk,hkd->hgqd", back_scores, key_low, preferred_element_type=jnp.float32)
        * score_scale
    ]
    grad_keys = grad_keys.at[:, :block_rows].add(
        jnp.einsum("hgqk,hgqd->hkd", back_scores, query_low, preferred_element_type=jnp.float32)
        * score_scale
    )
    value_gradients = value_gradients.at[:, :block_rows].add(
        jnp.einsum(
            "hgqk,hgqd->hkd",
            soft_weights.astype(jnp.bfloat16),
            heads_gradient,
            preferred_element_type=jnp.float32,
        )
    )
    return (jnp.concatenate(query_parts, axis=2), grad_keys, value_gradients)


def shards(
    tokens,
    cotangent,
    lengths,
    w_in,
    w_out,
    gains,
    first_in,
    first_out,
    gain_first,
    second_in,
    second_out,
    gain_second,
):
    slot_batch = lengths.shape[0]
    row_total = tokens.shape[0]
    query_group_width = QUERY_HEADS // KEY_VALUE_HEADS
    gathered_in, gathered_out, gathered_gains = (
        lax.all_gather(w_in.astype(jnp.bfloat16), "shard", axis=0, tiled=True),
        lax.all_gather(w_out.astype(jnp.bfloat16), "shard", axis=0, tiled=True),
        lax.all_gather(gains.astype(jnp.bfloat16), "shard", axis=0, tiled=True),
    )
    gain_all = gathered_gains.astype(jnp.float32)
    gain_in = gain_all[:MODEL_WIDTH]
    gain_post = gain_all[MODEL_WIDTH : 2 * MODEL_WIDTH]
    gain_query = gain_all[2 * MODEL_WIDTH : 2 * MODEL_WIDTH + HEAD_SIZE]
    gain_key = gain_all[2 * MODEL_WIDTH + HEAD_SIZE :]
    proj_qkv = gathered_in[:, :QKVC]
    proj_mix = gathered_in[:, QKVC:]
    proj_attn = gathered_out[: QUERY_HEADS * HEAD_SIZE]
    proj_down = gathered_out[QUERY_HEADS * HEAD_SIZE :]
    cosine, sine = rope_tables(SLOT_ROWS, HEAD_SIZE)
    layer_inputs = tokens.astype(jnp.float32)
    normed, pull_in = jax.vjp(rms_scale, layer_inputs, gain_in)
    normed_low = normed.astype(jnp.bfloat16)
    unnormed_rows = jnp.dot(normed_low, proj_qkv, preferred_element_type=jnp.float32).reshape(
        slot_batch, SLOT_ROWS, QKVC
    )

    def prep_local(raw_part, gain_q, gain_k):
        return prepare(raw_part, gain_q, gain_k, cosine, sine)

    (queries, key_head_rows, value_head_rows), pull_prep = jax.vjp(
        prep_local, unnormed_rows, gain_query, gain_key
    )
    query_low = (
        queries.astype(jnp.bfloat16)
        .reshape(slot_batch, SLOT_ROWS, KEY_VALUE_HEADS, query_group_width, HEAD_SIZE)
        .transpose(0, 2, 3, 1, 4)
    )
    key_low = key_head_rows.astype(jnp.bfloat16).transpose(0, 2, 1, 3)
    value_low = value_head_rows.astype(jnp.bfloat16).transpose(0, 2, 1, 3)
    attended, totals = lax.map(
        lambda slot_item: slot_attention(slot_item[0], slot_item[1], slot_item[2], slot_item[3]),
        (query_low, key_low, value_low, lengths),
    )
    attended_rows = attended.transpose(0, 3, 1, 2, 4).reshape(row_total, QUERY_HEADS * HEAD_SIZE)
    middle = layer_inputs + jnp.dot(attended_rows, proj_attn, preferred_element_type=jnp.float32)
    normed_post, pull_post = jax.vjp(rms_scale, middle, gain_post)
    post_low = normed_post.astype(jnp.bfloat16)
    mixed = jnp.dot(post_low, proj_mix, preferred_element_type=jnp.float32)
    hidden, pull_gate = jax.vjp(gated_unit, mixed)
    hidden_low = hidden.astype(jnp.bfloat16)
    layer_output = (
        middle + jnp.dot(hidden_low, proj_down, preferred_element_type=jnp.float32)
    ).astype(jnp.bfloat16)
    positions = jnp.arange(SLOT_ROWS, dtype=jnp.int32)
    valid_row_count = (
        (positions[None, :] < lengths[:, None]).astype(jnp.float32).reshape(row_total, 1)
    )
    back_out = cotangent.astype(jnp.float32) * valid_row_count
    back_out_low = back_out.astype(jnp.bfloat16)
    grad_down = outer_sum(hidden_low, back_out_low)
    back_hidden = back_product(back_out_low, proj_down)
    (back_mixed,) = pull_gate(back_hidden)
    mixed_low = back_mixed.astype(jnp.bfloat16)
    grad_mix = outer_sum(post_low, mixed_low)
    back_post = back_product(mixed_low, proj_mix)
    back_middle, grad_gain_post = pull_post(back_post)
    back_middle = back_middle + back_out
    middle_low = back_middle.astype(jnp.bfloat16)
    grad_attn = outer_sum(attended_rows, middle_low)
    attended_gradient = back_product(middle_low, proj_attn).astype(jnp.bfloat16)
    heads_gradient = attended_gradient.reshape(
        slot_batch, SLOT_ROWS, KEY_VALUE_HEADS, query_group_width, HEAD_SIZE
    ).transpose(0, 2, 3, 1, 4)
    grad_query, grad_key, grad_value = lax.map(
        lambda slot_item: slot_attention_back(
            slot_item[0], slot_item[1], slot_item[2], slot_item[3], slot_item[4], slot_item[5]
        ),
        (query_low, key_low, value_low, totals, heads_gradient, lengths),
    )
    grad_query = grad_query.transpose(0, 3, 1, 2, 4).reshape(
        slot_batch, SLOT_ROWS, QUERY_HEADS, HEAD_SIZE
    )
    grad_key = grad_key.transpose(0, 2, 1, 3)
    grad_value = grad_value.transpose(0, 2, 1, 3)
    back_raw, grad_gain_query, grad_gain_key = pull_prep((grad_query, grad_key, grad_value))
    raw_low = back_raw.reshape(row_total, QKVC).astype(jnp.bfloat16)
    grad_qkv = outer_sum(normed_low, raw_low)
    back_normed = back_product(raw_low, proj_qkv)
    back_inputs, grad_gain_in = pull_in(back_normed)
    layer_input_gradient = (back_middle + back_inputs).astype(jnp.bfloat16)
    output_values = layer_output.astype(jnp.float32)
    value_gradients = layer_input_gradient.astype(jnp.float32)
    sum_out, sum_grad, sum_count = lax.psum(
        (
            jnp.sum(valid_row_count * output_values * output_values),
            jnp.sum(valid_row_count * value_gradients * value_gradients),
            jnp.sum(valid_row_count),
        ),
        ("dp", "shard"),
    )
    valid_rms = jnp.sqrt(jnp.stack([sum_out, sum_grad]) / (sum_count * MODEL_WIDTH))
    owners = lax.axis_size("shard")
    grad_in = jnp.concatenate([grad_qkv, grad_mix], axis=1)
    grad_out = jnp.concatenate([grad_attn, grad_down], axis=0)
    grad_gain = jnp.concatenate(
        [grad_gain_in, grad_gain_post, grad_gain_query, grad_gain_key]
    ).reshape(owners, GN // owners)
    part_in, part_out, part_gain = (
        lax.psum_scatter(grad_in, "dp", scatter_dimension=1, tiled=True),
        lax.psum_scatter(grad_out, "dp", scatter_dimension=1, tiled=True),
        lax.psum_scatter(grad_gain, "dp", scatter_dimension=1, tiled=True),
    )
    owned_in, owned_out, owned_gain = (
        lax.psum_scatter(part_in, "shard", scatter_dimension=0, tiled=True),
        lax.psum_scatter(part_out, "shard", scatter_dimension=0, tiled=True),
        lax.psum_scatter(part_gain, "shard", scatter_dimension=0, tiled=True),
    )
    summed_in, summed_out, summed_gain = (
        lax.all_gather(owned_in, "dp", axis=1, tiled=True),
        lax.all_gather(owned_out, "dp", axis=1, tiled=True),
        lax.all_gather(owned_gain, "dp", axis=1, tiled=True),
    )
    summed_gain = summed_gain.reshape(-1)
    new_w_in, new_first_in, new_second_in = adamw_update(
        w_in, first_in, second_in, summed_in, MATRIX_RATE, MATRIX_DECAY
    )
    new_w_out, new_first_out, new_second_out = adamw_update(
        w_out, first_out, second_out, summed_out, MATRIX_RATE, MATRIX_DECAY
    )
    new_gains, new_gain_first, new_gain_second = adamw_update(
        gains, gain_first, gain_second, summed_gain, GAIN_RATE, 0.0
    )
    return (
        layer_output,
        layer_input_gradient,
        new_w_in,
        new_w_out,
        new_gains,
        new_first_in,
        new_first_out,
        new_gain_first,
        new_second_in,
        new_second_out,
        new_gain_second,
        valid_rms,
    )


def low(values):
    return values.astype(jnp.bfloat16)


def wide(values):
    return values.astype(jnp.float32)


def mul(left, right):
    return jnp.dot(left, right, preferred_element_type=jnp.float32)


def mul_bt(left, right):
    return lax.dot_general(
        left, right, (((1,), (1,)), ((), ())), preferred_element_type=jnp.float32
    )


def mul_at(left, right):
    return lax.dot_general(
        left, right, (((0,), (0,)), ((), ())), preferred_element_type=jnp.float32
    )


def whole(shape):
    return pl.BlockSpec(shape, lambda *_: (0,) * len(shape))


def shape_of(shape, kind):
    return jax.ShapeDtypeStruct(shape, kind)


BF = jnp.bfloat16
F32 = jnp.float32
VMEM_BYTES = 60 * 1024 * 1024


def params(axes=1):
    return pltpu.CompilerParams(
        dimension_semantics=("arbitrary",) * axes, vmem_limit_bytes=VMEM_BYTES
    )


def split_columns(values, core):
    half = values.shape[1] // 2
    first, second = values[:, :half], values[:, half:]
    mine = core == 0
    return jnp.where(mine, first, second), jnp.where(mine, second, first)


def join_columns(own, other, core):
    mine = core == 0
    return jnp.concatenate(
        [jnp.where(mine, own, other), jnp.where(mine, other, own)], axis=1
    )


def cast_qkv_kernel(q_ref, k_ref, v_ref, out_ref):
    out_ref[0, :, :256] = low(q_ref[...])
    out_ref[0, :, 256:384] = low(k_ref[...])
    out_ref[0, :, 384:] = low(v_ref[...])


def cast_qkv(w_in):
    rows = w_in.shape[0]
    return pl.pallas_call(
        cast_qkv_kernel,
        grid=(KEY_VALUE_HEADS,),
        in_specs=[
            pl.BlockSpec((rows, 256), lambda g: (0, g)),
            pl.BlockSpec((rows, 128), lambda g: (0, 16 + g)),
            pl.BlockSpec((rows, 128), lambda g: (0, 24 + g)),
        ],
        out_specs=pl.BlockSpec((1, rows, 512), lambda g: (g, 0, 0)),
        out_shape=shape_of((KEY_VALUE_HEADS, rows, 512), BF),
        compiler_params=params(),
        name="cast_qkv",
    )(w_in, w_in, w_in)


def cast_mix_kernel(gate_ref, up_ref, out_ref):
    out_ref[0, :, :FFB] = low(gate_ref[...])
    out_ref[0, :, FFB:] = low(up_ref[...])


FFB = 1024
FF_STEPS = FF // FFB


def cast_mix(w_in):
    rows = w_in.shape[0]
    return pl.pallas_call(
        cast_mix_kernel,
        grid=(FF_STEPS,),
        in_specs=[
            pl.BlockSpec((rows, FFB), lambda j: (0, QKVC // FFB + j)),
            pl.BlockSpec((rows, FFB), lambda j: (0, (QKVC + FF) // FFB + j)),
        ],
        out_specs=pl.BlockSpec((1, rows, 2 * FFB), lambda j: (j, 0, 0)),
        out_shape=shape_of((FF_STEPS, rows, 2 * FFB), BF),
        compiler_params=params(),
        name="cast_mix",
    )(w_in, w_in)


def turn(values):
    return pltpu.roll(values, HEAD_SIZE // 2, 1)


def head_norm(raw):
    scale = lax.rsqrt(jnp.mean(raw * raw, axis=-1, keepdims=True) + EPSILON)
    return raw * scale, scale


def block_mask(first_row, rows, keys, length):
    row = first_row + lax.broadcasted_iota(jnp.int32, (rows, keys), 0)
    key = lax.broadcasted_iota(jnp.int32, (rows, keys), 1)
    return (key <= row) & (key < length)


QB = 256


def forward_kernel(
    meta_ref,
    x_ref,
    gain_ref,
    head_gain_ref,
    cos_ref,
    sin_ref,
    own_ref,
    other_ref,
    o_ref,
    qkv_ref,
    u_ref,
    lse_ref,
    a_own_ref,
    a_other_ref,
):
    core, length = meta_ref[0], meta_ref[1]

    @pl.when(pl.program_id(0) == 0)
    def _():
        x = wide(x_ref[...])
        scale = lax.rsqrt(jnp.mean(x * x, axis=-1, keepdims=True) + EPSILON)
        own, other = split_columns(low(x * scale * gain_ref[...]), core)
        a_own_ref[...] = own
        a_other_ref[...] = other

    u = mul(a_own_ref[...], own_ref[0]) + mul(a_other_ref[...], other_ref[0])
    u_ref[0] = u[:, :384]
    cosine, sine = cos_ref[...], sin_ref[...]
    gain_q, gain_k = head_gain_ref[0:1, :], head_gain_ref[1:2, :]
    for part in range(3):
        normed, _ = head_norm(u[:, part * 128 : part * 128 + 128])
        normed = normed * (gain_k if part == 2 else gain_q)
        qkv_ref[0, :, part * 128 : part * 128 + 128] = low(
            normed * cosine + turn(normed) * sine
        )
    qkv_ref[0, :, 384:] = low(u[:, 384:])
    score_scale = HEAD_SIZE ** (-0.5)
    for head in range(2):
        for first in range(0, SLOT_ROWS, QB):
            keys = first + QB
            rows = slice(first, first + QB)
            q = qkv_ref[0, rows, head * 128 : head * 128 + 128]
            k = qkv_ref[0, :keys, 256:384]
            v = qkv_ref[0, :keys, 384:]
            scores = mul_bt(q, k) * score_scale
            scores = jnp.where(block_mask(first, QB, keys, length), scores, NEG_LARGE)
            peak = jnp.max(scores, axis=-1, keepdims=True)
            powers = jnp.exp(scores - peak)
            total = jnp.sum(powers, axis=-1, keepdims=True)
            soft = low(powers * (1.0 / total))
            o_ref[rows, head * 128 : head * 128 + 128] = low(mul(soft, v))
            lse_ref[0, rows, head * 128 : head * 128 + 128] = jnp.broadcast_to(
                peak + jnp.log(total), (QB, 128)
            )


def forward(meta, tokens, gain_in, head_gains, cosine, sine, own, other):
    rows = SLOT_ROWS
    half = MODEL_WIDTH // 2
    return pl.pallas_call(
        forward_kernel,
        grid_spec=pltpu.PrefetchScalarGridSpec(
            num_scalar_prefetch=1,
            grid=(KEY_VALUE_HEADS,),
            in_specs=[
                whole((rows, MODEL_WIDTH)),
                whole((1, MODEL_WIDTH)),
                whole((2, HEAD_SIZE)),
                whole((rows, HEAD_SIZE)),
                whole((rows, HEAD_SIZE)),
                pl.BlockSpec((1, half, 512), lambda g, _: (g, 0, 0)),
                pl.BlockSpec((1, half, 512), lambda g, _: (g, 0, 0)),
            ],
            out_specs=[
                pl.BlockSpec((rows, 256), lambda g, _: (0, g)),
                pl.BlockSpec((1, rows, 512), lambda g, _: (g, 0, 0)),
                pl.BlockSpec((1, rows, 384), lambda g, _: (g, 0, 0)),
                pl.BlockSpec((1, rows, 256), lambda g, _: (g, 0, 0)),
                whole((rows, half)),
                whole((rows, half)),
            ],
        ),
        out_shape=[
            shape_of((rows, QUERY_HEADS * HEAD_SIZE), BF),
            shape_of((KEY_VALUE_HEADS, rows, 512), BF),
            shape_of((KEY_VALUE_HEADS, rows, 384), F32),
            shape_of((KEY_VALUE_HEADS, rows, 256), F32),
            shape_of((rows, half), BF),
            shape_of((rows, half), BF),
        ],
        compiler_params=params(),
        cost_estimate=pl.CostEstimate(
            flops=7_000_000_000, bytes_accessed=24_000_000, transcendentals=5_000_000
        ),
        name="forward",
    )(meta, tokens, gain_in, head_gains, cosine, sine, own, other)


def unit_kernel(
    meta_ref,
    o_ref,
    x_ref,
    cot_ref,
    gain_ref,
    wo_ref,
    wd_ref,
    own_ref,
    other_ref,
    y_ref,
    dm_ref,
    b_own_ref,
    b_other_ref,
    left_ref,
    send_ref,
    e_ref,
    right_ref,
    right_send_ref,
    dmid_ref,
    dlow_ref,
    small_ref,
    mid_s,
    y_s,
    db_own_s,
    db_other_s,
):
    core, length = meta_ref[0], meta_ref[1]
    step = pl.program_id(0)
    attended = QUERY_HEADS * HEAD_SIZE
    valid = lax.broadcasted_iota(jnp.int32, (SLOT_ROWS, 1), 0) < length

    @pl.when(step == 0)
    def _():
        e_ref[...] = jnp.where(valid, cot_ref[...], jnp.zeros((), BF))
        middle = wide(x_ref[...]) + mul(o_ref[...], wo_ref[...])
        mid_s[...] = middle
        y_s[...] = middle
        scale = lax.rsqrt(jnp.mean(middle * middle, axis=-1, keepdims=True) + EPSILON)
        own, other = split_columns(low(middle * scale * gain_ref[...]), core)
        b_own_ref[...] = own
        b_other_ref[...] = other
        db_own_s[...] = jnp.zeros_like(db_own_s)
        db_other_s[...] = jnp.zeros_like(db_other_s)

        @pl.when(core == 0)
        def _():
            left_ref[:, :attended] = o_ref[...]

        @pl.when(core != 0)
        def _():
            send_ref[:, :attended] = o_ref[...]

    e = e_ref[...]
    gu = mul(b_own_ref[...], own_ref[0]) + mul(b_other_ref[...], other_ref[0])
    gate, up = gu[:, :FFB], gu[:, FFB:]
    sigma = 1.0 / (1.0 + jnp.exp(-gate))
    silu = gate * sigma
    hidden = low(silu * up)
    down = wd_ref[...]
    y_s[...] += mul(hidden, down)
    dh = mul_bt(e, down)
    dm = jnp.concatenate(
        [low(dh * up * (sigma * (1.0 + gate * (1.0 - sigma)))), low(dh * silu)], axis=1
    )
    dm_ref[...] = dm
    db_own_s[...] += mul_bt(dm, own_ref[0])
    db_other_s[...] += mul_bt(dm, other_ref[0])

    for now in range(FF_STEPS):

        @pl.when(step == now)
        def _():
            if now == 0:

                @pl.when(core == 0)
                def _():
                    left_ref[:, attended:] = hidden[:, :512]
                    send_ref[:, :512] = hidden[:, 512:]

                @pl.when(core != 0)
                def _():
                    send_ref[:, attended:] = hidden[:, :512]
                    left_ref[:, :512] = hidden[:, 512:]

            else:
                at = slice(now * FFB - 512, now * FFB - 512 + FFB)

                @pl.when(core == 0)
                def _():
                    send_ref[:, at] = hidden

                @pl.when(core != 0)
                def _():
                    left_ref[:, at] = hidden

    @pl.when(step == FF_STEPS - 1)
    def _():
        y = low(y_s[...])
        y_ref[...] = y
        y = wide(y)
        total = jnp.sum(jnp.where(valid, y * y, 0.0))
        db = join_columns(db_own_s[...], db_other_s[...], core)
        middle = mid_s[...]
        scale = lax.rsqrt(jnp.mean(middle * middle, axis=-1, keepdims=True) + EPSILON)
        normed = middle * scale
        dn = db * gain_ref[...]
        dmid = wide(e) + scale * (
            dn - normed * jnp.mean(dn * normed, axis=-1, keepdims=True)
        )
        dmid_ref[...] = dmid
        dlow = low(dmid)
        dlow_ref[...] = dlow
        mine = core == 0
        right_ref[...] = jnp.where(mine, dlow, e)
        right_send_ref[...] = jnp.where(mine, e, dlow)
        small_ref[0:1, :] = jnp.sum(db * normed, axis=0, keepdims=True)
        small_ref[1:8, :] = jnp.full((7, MODEL_WIDTH), total)


def unit(meta, o, tokens, cotangent, gain_post, w_out, own, other):
    rows = SLOT_ROWS
    half = MODEL_WIDTH // 2
    attended = QUERY_HEADS * HEAD_SIZE
    owned = w_out.shape[0] // 2
    return pl.pallas_call(
        unit_kernel,
        grid_spec=pltpu.PrefetchScalarGridSpec(
            num_scalar_prefetch=1,
            grid=(FF_STEPS,),
            in_specs=[
                whole((rows, attended)),
                whole((rows, MODEL_WIDTH)),
                whole((rows, MODEL_WIDTH)),
                whole((1, MODEL_WIDTH)),
                pl.BlockSpec((attended, MODEL_WIDTH), lambda j, _: (0, 0)),
                pl.BlockSpec((FFB, MODEL_WIDTH), lambda j, _: (attended // FFB + j, 0)),
                pl.BlockSpec((1, half, 2 * FFB), lambda j, _: (j, 0, 0)),
                pl.BlockSpec((1, half, 2 * FFB), lambda j, _: (j, 0, 0)),
            ],
            out_specs=[
                whole((rows, MODEL_WIDTH)),
                pl.BlockSpec((rows, 2 * FFB), lambda j, _: (0, j)),
                whole((rows, half)),
                whole((rows, half)),
                whole((rows, owned)),
                whole((rows, owned)),
                whole((rows, MODEL_WIDTH)),
                whole((rows, MODEL_WIDTH)),
                whole((rows, MODEL_WIDTH)),
                whole((rows, MODEL_WIDTH)),
                whole((rows, MODEL_WIDTH)),
                whole((8, MODEL_WIDTH)),
            ],
            scratch_shapes=[
                pltpu.VMEM((rows, MODEL_WIDTH), F32),
                pltpu.VMEM((rows, MODEL_WIDTH), F32),
                pltpu.VMEM((rows, half), F32),
                pltpu.VMEM((rows, half), F32),
            ],
        ),
        out_shape=[
            shape_of((rows, MODEL_WIDTH), BF),
            shape_of((rows, 2 * FF), BF),
            shape_of((rows, half), BF),
            shape_of((rows, half), BF),
            shape_of((rows, owned), BF),
            shape_of((rows, owned), BF),
            shape_of((rows, MODEL_WIDTH), BF),
            shape_of((rows, MODEL_WIDTH), BF),
            shape_of((rows, MODEL_WIDTH), BF),
            shape_of((rows, MODEL_WIDTH), F32),
            shape_of((rows, MODEL_WIDTH), BF),
            shape_of((8, MODEL_WIDTH), F32),
        ],
        compiler_params=params(),
        cost_estimate=pl.CostEstimate(
            flops=21_500_000_000, bytes_accessed=50_000_000, transcendentals=2_000_000
        ),
        name="unit",
    )(meta, o, tokens, cotangent, gain_post, w_out, w_out, own, other)


def backward_kernel(
    meta_ref,
    dmid_ref,
    dlow_ref,
    x_ref,
    gain_ref,
    head_gain_ref,
    cos_ref,
    sin_ref,
    wo_ref,
    own_ref,
    other_ref,
    qkv_ref,
    u_ref,
    lse_ref,
    small_in_ref,
    dx_ref,
    du_ref,
    small_ref,
    da_own_s,
    da_other_s,
    head_s,
    dk_s,
    dv_s,
):
    core, length = meta_ref[0], meta_ref[1]
    group = pl.program_id(0)

    @pl.when(group == 0)
    def _():
        da_own_s[...] = jnp.zeros_like(da_own_s)
        da_other_s[...] = jnp.zeros_like(da_other_s)
        head_s[...] = jnp.zeros_like(head_s)

    cosine, sine = cos_ref[...], sin_ref[...]
    score_scale = HEAD_SIZE ** (-0.5)
    do = low(mul_bt(dlow_ref[...], wo_ref[...]))

    def through(grad, raw, gain, slot):
        back = grad * cosine - turn(grad) * sine
        normed, scale = head_norm(raw)
        head_s[slot : slot + 1, :] += jnp.sum(back * normed, axis=0, keepdims=True)
        dn = back * gain
        return low(scale * (dn - normed * jnp.mean(dn * normed, axis=-1, keepdims=True)))

    parts = []
    for head in range(2):
        columns = slice(head * 128, head * 128 + 128)
        grad_rows = []
        for first in range(0, SLOT_ROWS, QB):
            keys = first + QB
            rows = slice(first, first + QB)
            q = qkv_ref[0, rows, columns]
            k = qkv_ref[0, :keys, 256:384]
            v = qkv_ref[0, :keys, 384:]
            dos = do[rows, columns]
            scores = mul_bt(q, k) * score_scale
            soft = jnp.where(
                block_mask(first, QB, keys, length),
                jnp.exp(scores - lse_ref[0, rows, head * 128 : head * 128 + 1]),
                0.0,
            )
            dsoft = mul_bt(dos, v)
            inner = jnp.sum(soft * dsoft, axis=-1, keepdims=True)
            ds = low(soft * (dsoft - inner))
            grad_rows.append(mul(ds, k))
            grad_k = mul_at(ds, q)
            grad_v = mul_at(low(soft), dos)
            last = first + QB == SLOT_ROWS
            if head == 0 and last:
                dk_s[...] = grad_k
                dv_s[...] = grad_v
                for keys_before, gk, gv in before:
                    dk_s[:keys_before, :] += gk
                    dv_s[:keys_before, :] += gv
            elif head == 0:
                if first == 0:
                    before = []
                before.append((keys, grad_k, grad_v))
            else:
                dk_s[:keys, :] += grad_k
                dv_s[:keys, :] += grad_v
        grad_q = jnp.concatenate(grad_rows, axis=0) * score_scale
        parts.append(through(grad_q, u_ref[0, :, columns], head_gain_ref[0:1, :], 0))
    parts.append(
        through(dk_s[...] * score_scale, u_ref[0, :, 256:384], head_gain_ref[1:2, :], 1)
    )
    parts.append(low(dv_s[...]))
    du = jnp.concatenate(parts, axis=1)
    du_ref[:, pl.ds(pl.multiple_of(group * 256, 256), 256)] = du[:, :256]
    du_ref[:, pl.ds(pl.multiple_of(2048 + group * 128, 128), 128)] = du[:, 256:384]
    du_ref[:, pl.ds(pl.multiple_of(3072 + group * 128, 128), 128)] = du[:, 384:]
    da_own_s[...] += mul_bt(du, own_ref[0])
    da_other_s[...] += mul_bt(du, other_ref[0])

    @pl.when(group == KEY_VALUE_HEADS - 1)
    def _():
        da = join_columns(da_own_s[...], da_other_s[...], core)
        x = wide(x_ref[...])
        scale = lax.rsqrt(jnp.mean(x * x, axis=-1, keepdims=True) + EPSILON)
        normed = x * scale
        dn = da * gain_ref[...]
        dx = low(
            dmid_ref[...]
            + scale * (dn - normed * jnp.mean(dn * normed, axis=-1, keepdims=True))
        )
        dx_ref[...] = dx
        dx = wide(dx)
        valid = lax.broadcasted_iota(jnp.int32, (SLOT_ROWS, 1), 0) < length
        total = jnp.sum(jnp.where(valid, dx * dx, 0.0))
        small_ref[0:1, :] = jnp.sum(da * normed, axis=0, keepdims=True)
        small_ref[1:2, :] = small_in_ref[0:1, :]
        small_ref[2:8, :] = jnp.full((6, MODEL_WIDTH), total)
        small_ref[2:3, 0:128] = head_s[0:1, :]
        small_ref[2:3, 128:256] = head_s[1:2, :]
        small_ref[3:4, :] = small_in_ref[1:2, :]
        small_ref[4:5, :] = jnp.full((1, MODEL_WIDTH), 1.0) * length.astype(F32)


def backward(
    meta, dmid, dlow, tokens, gain_in, head_gains, cosine, sine, w_out, own, other, qkv, u, lse, small
):
    rows = SLOT_ROWS
    half = MODEL_WIDTH // 2
    return pl.pallas_call(
        backward_kernel,
        grid_spec=pltpu.PrefetchScalarGridSpec(
            num_scalar_prefetch=1,
            grid=(KEY_VALUE_HEADS,),
            in_specs=[
                whole((rows, MODEL_WIDTH)),
                whole((rows, MODEL_WIDTH)),
                whole((rows, MODEL_WIDTH)),
                whole((1, MODEL_WIDTH)),
                whole((2, HEAD_SIZE)),
                whole((rows, HEAD_SIZE)),
                whole((rows, HEAD_SIZE)),
                pl.BlockSpec((256, MODEL_WIDTH), lambda g, _: (g, 0)),
                pl.BlockSpec((1, half, 512), lambda g, _: (g, 0, 0)),
                pl.BlockSpec((1, half, 512), lambda g, _: (g, 0, 0)),
                pl.BlockSpec((1, rows, 512), lambda g, _: (g, 0, 0)),
                pl.BlockSpec((1, rows, 384), lambda g, _: (g, 0, 0)),
                pl.BlockSpec((1, rows, 256), lambda g, _: (g, 0, 0)),
                whole((8, MODEL_WIDTH)),
            ],
            out_specs=[
                whole((rows, MODEL_WIDTH)),
                whole((rows, QKVC)),
                whole((8, MODEL_WIDTH)),
            ],
            scratch_shapes=[
                pltpu.VMEM((rows, half), F32),
                pltpu.VMEM((rows, half), F32),
                pltpu.VMEM((8, HEAD_SIZE), F32),
                pltpu.VMEM((rows, HEAD_SIZE), F32),
                pltpu.VMEM((rows, HEAD_SIZE), F32),
            ],
        ),
        out_shape=[
            shape_of((rows, MODEL_WIDTH), BF),
            shape_of((rows, QKVC), BF),
            shape_of((8, MODEL_WIDTH), F32),
        ],
        compiler_params=params(),
        cost_estimate=pl.CostEstimate(
            flops=12_000_000_000, bytes_accessed=35_000_000, transcendentals=5_000_000
        ),
        name="backward",
    )(meta, dmid, dlow, tokens, gain_in, head_gains, cosine, sine, w_out, own, other, qkv, u, lse, small)


def grad_in_kernel(meta_ref, l_own, l_got, r_own, r_got, keep_ref, send_ref, acc):
    rank = meta_ref[2]
    acc[...] = mul_at(l_own[...], r_own[...]) + mul_at(l_got[...], r_got[...])
    piece = acc.shape[0] // PIECES
    for at in range(PIECES):
        source = pl.multiple_of(lax.bitwise_xor(at, rank) * piece, piece)
        target, place = (
            (keep_ref, at) if at < PIECES // 2 else (send_ref, at - PIECES // 2)
        )
        target[place * piece : (place + 1) * piece, :] = low(acc[pl.ds(source, piece), :])


PIECES = 16


def grad_in(meta, l_own, l_got, r_own, r_got, first, count, block):
    rows = l_own.shape[1]
    tokens = l_own.shape[0]
    half = shape_of((rows // 2, count * block), BF)
    out = pl.BlockSpec((rows // 2, block), lambda j, _: (0, j))
    right = pl.BlockSpec((tokens, block), lambda j, _: (0, first + j))
    return pl.pallas_call(
        grad_in_kernel,
        grid_spec=pltpu.PrefetchScalarGridSpec(
            num_scalar_prefetch=1,
            grid=(count,),
            in_specs=[whole((tokens, rows)), whole((tokens, rows)), right, right],
            out_specs=[out, out],
            scratch_shapes=[pltpu.VMEM((rows, block), F32)],
        ),
        out_shape=[half, half],
        compiler_params=params(),
        cost_estimate=pl.CostEstimate(
            flops=4 * tokens * rows * count * block,
            bytes_accessed=2 * count * block * (2 * tokens + rows),
            transcendentals=0,
        ),
        name="grad_in",
    )(meta, l_own, l_got, r_own, r_got)


def grad_out_kernel(
    meta_ref, l_own, l_got, r_own, r_got, e_own, e_got, keep_ref, send_ref, acc
):
    rank = meta_ref[2]
    relative = pl.program_id(0)
    top = rank // (PIECES // 2)
    half = jnp.where(relative == 0, 1 - top, top)
    attended = QUERY_HEADS * HEAD_SIZE
    rows = acc.shape[0]
    rest = attended - rows

    @pl.when(half == 0)
    def _():
        acc[...] = mul_at(l_own[...], r_own[...]) + mul_at(l_got[...], r_got[...])

    @pl.when(half != 0)
    def _():
        acc[:rest, :] = mul_at(l_own[:, :rest], r_own[...]) + mul_at(l_got[:, :rest], r_got[...])
        acc[rest:, :] = mul_at(l_own[:, rest:], e_own[...]) + mul_at(l_got[:, rest:], e_got[...])

    inner = lax.rem(rank, PIECES // 2)
    piece = rows // (PIECES // 2)

    def store(target):
        for at in range(PIECES // 2):
            source = pl.multiple_of(lax.bitwise_xor(at, inner) * piece, piece)
            target[at * piece : (at + 1) * piece, :] = low(acc[pl.ds(source, piece), :])

    @pl.when(relative == 0)
    def _():
        store(send_ref)

    @pl.when(relative != 0)
    def _():
        store(keep_ref)


def grad_out(meta, l_own, l_got, r_own, r_got, e_own, e_got):
    tokens, rows = l_own.shape
    block = 512
    steps = MODEL_WIDTH // block
    half = shape_of((rows // 2, MODEL_WIDTH), BF)

    def left_at(r, j, meta_ref):
        top = meta_ref[2] // (PIECES // 2)
        return (0, jnp.where(r == 0, 1 - top, top))

    left = pl.BlockSpec((tokens, rows // 2), left_at)
    right = pl.BlockSpec((tokens, block), lambda r, j, _: (0, j))
    return pl.pallas_call(
        grad_out_kernel,
        grid_spec=pltpu.PrefetchScalarGridSpec(
            num_scalar_prefetch=1,
            grid=(2, steps),
            in_specs=[left, left, right, right, right, right],
            out_specs=[
                pl.BlockSpec((rows // 2, block), lambda r, j, _: (0, r * j)),
                pl.BlockSpec(
                    (rows // 2, block), lambda r, j, _: (0, jnp.where(r == 0, j, steps - 1))
                ),
            ],
            scratch_shapes=[pltpu.VMEM((rows // 2, block), F32)],
        ),
        out_shape=[half, half],
        compiler_params=params(2),
        cost_estimate=pl.CostEstimate(
            flops=4 * tokens * rows * MODEL_WIDTH,
            bytes_accessed=20_000_000,
            transcendentals=0,
        ),
        name="grad_out",
    )(meta, l_own, l_got, r_own, r_got, e_own, e_got)


class Ring:
    def __init__(self, chips, cores):
        bits = chips.bit_length() - 1
        self.bits = bits
        order = list(range(bits))
        even = [0, 2, 1] + order[3:] if bits >= 3 else order
        odd = [1, 2, 0] + order[3:] if bits >= 3 else order[::-1]
        self.orders = [even, odd]
        self.cores = cores
        self.chips = chips

    def rank(self, chip, core):
        def code(order):
            value = 0
            for stage, bit in enumerate(order):
                value = value + (((chip >> bit) & 1) << (self.bits - 1 - stage))
            return value

        return jnp.where(core % 2 == 0, code(self.orders[0]), code(self.orders[1]))

    def swap(self, values, stage):
        pairs = [
            (chip * self.cores + core, (chip ^ (1 << self.orders[core % 2][stage])) * self.cores + core)
            for chip in range(self.chips)
            for core in range(self.cores)
        ]
        return lax.ppermute(values, ("dp", "shard"), pairs)

    def scatter(self, keep, send):
        for stage in range(self.bits):
            got = self.swap(send, stage)
            half = keep.shape[0] // 2
            if stage == self.bits - 1:
                return low(wide(keep) + wide(got))
            keep, send = (
                low(wide(keep[:half]) + wide(got[:half])),
                low(wide(keep[half:]) + wide(got[half:])),
            )

    def gather(self, mine):
        for stage in range(self.bits - 1, 0, -1):
            mine = jnp.concatenate([mine, self.swap(mine, stage)], axis=0)
        return mine, self.swap(mine, 0)


def adam(weight, first, second, gradient, rate, decay):
    first = BETA_ONE * first + (1.0 - BETA_ONE) * gradient
    second = BETA_TWO * second + (1.0 - BETA_TWO) * gradient * gradient
    step = (first * (1.0 / (1.0 - BETA_ONE**STEP))) / (
        jnp.sqrt(second * (1.0 / (1.0 - BETA_TWO**STEP))) + ADAM_EPSILON
    )
    return weight - rate * (step + decay * weight), first, second


def adam_in_kernel(meta_ref, g_ref, w_ref, f_ref, s_ref, *rest):
    new_w, new_f, new_s = rest[-3:]
    count = PIECES // 2
    piece = g_ref.shape[0] // count
    inner = lax.rem(meta_ref[2], count)
    for at in range(count):
        source = pl.multiple_of(lax.bitwise_xor(at, inner) * piece, piece)
        there = slice(at * piece, (at + 1) * piece)
        new_w[there, :], new_f[there, :], new_s[there, :] = adam(
            w_ref[there, :],
            f_ref[there, :],
            s_ref[there, :],
            wide(g_ref[pl.ds(source, piece), :]),
            MATRIX_RATE,
            MATRIX_DECAY,
        )


def adam_out_kernel(meta_ref, g_ref, w_ref, f_ref, s_ref, *rest):
    new_w, new_f, new_s = rest[-3:]
    new_w[...], new_f[...], new_s[...] = adam(
        w_ref[...], f_ref[...], s_ref[...], wide(g_ref[...]), MATRIX_RATE, MATRIX_DECAY
    )


def adam_call(kernel, name, meta, gradient, states, done, grid, g_spec, spec):
    whole_shape = shape_of(states[0].shape, F32)
    return pl.pallas_call(
        kernel,
        grid_spec=pltpu.PrefetchScalarGridSpec(
            num_scalar_prefetch=1,
            grid=grid,
            in_specs=[g_spec, spec, spec, spec]
            + [pl.BlockSpec(memory_space=pl.ANY)] * len(done),
            out_specs=[spec, spec, spec],
        ),
        out_shape=[whole_shape] * 3,
        input_output_aliases={5 + i: i for i in range(len(done))},
        compiler_params=params(),
        cost_estimate=pl.CostEstimate(
            flops=20 * gradient.size, bytes_accessed=26 * gradient.size, transcendentals=0
        ),
        name=name,
    )(meta, gradient, *states, *done)


def half_of(meta_ref, received):
    top = meta_ref[2] // (PIECES // 2)
    return 1 - top if received else top


def adam_in(meta, gradient, states, done, received, place, block=1024):
    rows, columns = gradient.shape
    return adam_call(
        adam_in_kernel,
        "adam_in",
        meta,
        gradient,
        states,
        done,
        (columns // block,),
        pl.BlockSpec((rows, block), lambda j, _: (0, j)),
        pl.BlockSpec((rows, block), lambda j, m: (half_of(m, received), place(j))),
    )


def adam_out(meta, gradient, states, done, received):
    rows, columns = gradient.shape
    count = PIECES // 2
    return adam_call(
        adam_out_kernel,
        "adam_out",
        meta,
        gradient,
        states,
        done,
        (count,),
        pl.BlockSpec((rows // count, columns), lambda i, _: (i, 0)),
        pl.BlockSpec(
            (rows // count, columns),
            lambda i, m: (
                half_of(m, received) * count + lax.bitwise_xor(i, lax.rem(m[2], count)),
                0,
            ),
        ),
    )


def qkv_place(j):
    return j


def mix_place(j):
    return QKVC // FFB + j // 2 + lax.rem(j, 2) * FF_STEPS


def rope_constants():
    index = np.arange(HEAD_SIZE // 2, dtype=np.float32)
    frequency = np.exp(index * np.float32(-2.0 * math.log(1000000.0) / HEAD_SIZE))
    angles = np.arange(SLOT_ROWS, dtype=np.float32)[:, None] * frequency[None, :]
    cosine, sine = np.cos(angles), np.sin(angles)
    return (
        np.concatenate([cosine, cosine], axis=1).astype(np.float32),
        np.concatenate([-sine, sine], axis=1).astype(np.float32),
    )


def core_swap(values):
    return lax.ppermute(values, "shard", [(0, 1), (1, 0)])


def slot_shards(
    tokens,
    cotangent,
    lengths,
    w_in,
    w_out,
    gains,
    first_in,
    first_out,
    gain_first,
    second_in,
    second_out,
    gain_second,
):
    chip, core = lax.axis_index("dp"), lax.axis_index("shard")
    ring = Ring(lax.axis_size("dp"), lax.axis_size("shard"))
    rank = ring.rank(chip, core)
    meta = jnp.stack([core, lengths[0], rank, chip]).astype(jnp.int32)

    qkv_own = cast_qkv(w_in)
    qkv_other = core_swap(qkv_own)
    out_all = lax.all_gather(low(w_out), "shard", axis=0, tiled=True)
    mix_own = cast_mix(w_in)
    mix_other = core_swap(mix_own)
    gains_own = low(gains).reshape(1, -1)
    gains_other = core_swap(gains_own)
    gain_all = wide(join_columns(gains_own, gains_other, core))
    gain_in = gain_all[:, :MODEL_WIDTH]
    gain_post = gain_all[:, MODEL_WIDTH : 2 * MODEL_WIDTH]
    head_gains = gain_all[:, 2 * MODEL_WIDTH :].reshape(2, HEAD_SIZE)
    cosine, sine = (jnp.asarray(table) for table in rope_constants())

    o, qkv, u, lse, a_own, a_other = forward(
        meta, tokens, gain_in, head_gains, cosine, sine, qkv_own, qkv_other
    )
    y, dm, b_own, b_other, left, send, e, right, right_send, dmid, dlow, small = unit(
        meta, o, tokens, cotangent, gain_post, out_all, mix_own, mix_other
    )
    left_got, right_got, e_got = core_swap(send), core_swap(right_send), core_swap(e)
    dm_got, b_got = core_swap(dm), core_swap(b_other)
    part_out = ring.scatter(*grad_out(meta, left, left_got, right, right_got, e, e_got))
    part_mix = ring.scatter(*grad_in(meta, b_own, b_got, dm, dm_got, 0, 2 * FF // 1024, 1024))
    dx, du, small = backward(
        meta,
        dmid,
        dlow,
        tokens,
        gain_in,
        head_gains,
        cosine,
        sine,
        out_all,
        qkv_own,
        qkv_other,
        qkv,
        u,
        lse,
        small,
    )
    a_got, du_got = core_swap(a_other), core_swap(du)
    part_qkv = ring.scatter(*grad_in(meta, a_own, a_got, du, du_got, 0, QKVC // 1024, 1024))

    small = small + core_swap(small)
    for stage in range(ring.bits):
        small = small + ring.swap(small, stage)
    valid_rms = jnp.sqrt(
        jnp.stack([small[3, 0], small[2, 512]]) / (small[4, 0] * MODEL_WIDTH)
    )
    gain_sum = lax.dynamic_slice_in_dim(
        jnp.concatenate([small[0], small[1], small[2, :256]]), core * gains.shape[0], gains.shape[0]
    )
    new_gains, new_gain_first, new_gain_second = adam(
        gains, gain_first, gain_second, gain_sum, GAIN_RATE, 0.0
    )

    out_halves = ring.gather(part_out)
    mix_halves = ring.gather(part_mix)
    qkv_halves = ring.gather(part_qkv)
    states_out = (w_out, first_out, second_out)
    states_in = (w_in, first_in, second_in)
    new_out, new_in = (), ()
    for received in range(2):
        new_out = adam_out(meta, out_halves[received], states_out, new_out, received)
    for received in range(2):
        new_in = adam_in(meta, mix_halves[received], states_in, new_in, received, mix_place)
    for received in range(2):
        new_in = adam_in(meta, qkv_halves[received], states_in, new_in, received, qkv_place)
    return (
        y,
        dx,
        new_in[0],
        new_out[0],
        new_gains,
        new_in[1],
        new_out[1],
        new_gain_first,
        new_in[2],
        new_out[2],
        new_gain_second,
        valid_rms,
    )


def solution(mesh):
    in_specs = (
        P(("dp", "shard"), None),
        P(("dp", "shard"), None),
        P(("dp", "shard")),
        P("shard", None),
        P("shard", None),
        P("shard"),
        P("shard", None),
        P("shard", None),
        P("shard"),
        P("shard", None),
        P("shard", None),
        P("shard"),
    )
    out_specs = (
        P(("dp", "shard"), None),
        P(("dp", "shard"), None),
        P("shard", None),
        P("shard", None),
        P("shard"),
        P("shard", None),
        P("shard", None),
        P("shard"),
        P("shard", None),
        P("shard", None),
        P("shard"),
        P(),
    )
    chips, cores = mesh.shape["dp"], mesh.shape["shard"]
    program = slot_shards if cores == 2 and chips == PIECES else shards
    return jax.shard_map(program, mesh=mesh, in_specs=in_specs, out_specs=out_specs, check_vma=False)
```

```python
import functools
import math

import jax
import jax.numpy as jnp
import numpy as np
from jax import lax
from jax.experimental import pallas as pl
from jax.experimental.pallas import tpu as pltpu
from jax.sharding import PartitionSpec as P

MODEL_WIDTH = 1024
FF = 3072
QUERY_HEADS = 16
KEY_VALUE_HEADS = 8
HEAD_SIZE = 128
SLOT_ROWS = 512
STEP = 7
QKVC = 4096
GN = 2304


EPSILON = 1e-06
BETA_ONE = 0.9
BETA_TWO = 0.95
ADAM_EPSILON = 1e-08
MATRIX_RATE = 0.05
GAIN_RATE = 0.3
MATRIX_DECAY = 0.1
NEG_LARGE = -1e30


def rms_scale(values, gain):
    return values * lax.rsqrt(jnp.mean(values * values, axis=-1, keepdims=True) + EPSILON) * gain


def rope_tables(length, size):
    positions = jnp.arange(length, dtype=jnp.float32)
    half_index = jnp.arange(size // 2, dtype=jnp.float32)
    frequency = jnp.exp(half_index * (-2.0 * math.log(1000000.0) / size))
    angles = positions[:, None] * frequency[None, :]
    angles = jnp.concatenate([angles, angles], axis=1)
    return (jnp.cos(angles), jnp.sin(angles))


def rotate(values, cosine, sine):
    half_size = values.shape[-1] // 2
    turned = jnp.concatenate([-values[..., half_size:], values[..., :half_size]], axis=-1)
    return values * cosine[:, None, :] + turned * sine[:, None, :]


def prepare(unnormed_rows, gain_q, gain_k, cosine, sine):
    leading_rows = unnormed_rows.shape[:-1]
    queries = unnormed_rows[..., : QUERY_HEADS * HEAD_SIZE].reshape(
        leading_rows + (QUERY_HEADS, HEAD_SIZE)
    )
    key_head_rows = unnormed_rows[
        ..., QUERY_HEADS * HEAD_SIZE : (QUERY_HEADS + KEY_VALUE_HEADS) * HEAD_SIZE
    ].reshape(leading_rows + (KEY_VALUE_HEADS, HEAD_SIZE))
    value_head_rows = unnormed_rows[..., (QUERY_HEADS + KEY_VALUE_HEADS) * HEAD_SIZE :].reshape(
        leading_rows + (KEY_VALUE_HEADS, HEAD_SIZE)
    )
    queries = rotate(rms_scale(queries, gain_q), cosine, sine)
    key_head_rows = rotate(rms_scale(key_head_rows, gain_k), cosine, sine)
    return (queries, key_head_rows, value_head_rows)


def gated_unit(mixed):
    return jax.nn.silu(mixed[..., :FF]) * mixed[..., FF:]


def adamw_update(weight, first, second, gradient, rate, decay):
    first = BETA_ONE * first + (1.0 - BETA_ONE) * gradient
    second = BETA_TWO * second + (1.0 - BETA_TWO) * gradient * gradient
    corr_one = 1.0 - BETA_ONE**STEP
    corr_two = 1.0 - BETA_TWO**STEP
    update = first / corr_one / (jnp.sqrt(second / corr_two) + ADAM_EPSILON) + decay * weight
    return (weight - rate * update, first, second)


def outer_sum(left, right):
    return lax.dot_general(
        left, right, (((0,), (0,)), ((), ())), preferred_element_type=jnp.float32
    )


def back_product(gradient, weight):
    return lax.dot_general(
        gradient, weight, (((1,), (1,)), ((), ())), preferred_element_type=jnp.float32
    )


def key_mask(row_count, key_reach, length):
    query_pos = jnp.arange(row_count, dtype=jnp.int32)
    key_pos = jnp.arange(key_reach, dtype=jnp.int32)
    return (key_pos[None, :] <= query_pos[:, None]) & (key_pos[None, :] < length)


def slot_attention(query_low, key_low, value_low, length):
    block_rows = min(512, SLOT_ROWS)
    score_scale = HEAD_SIZE ** (-0.5)
    scores = (
        jnp.einsum("hgqd,hkd->hgqk", query_low, key_low, preferred_element_type=jnp.float32)
        * score_scale
    )
    scores = jnp.where(key_mask(block_rows, block_rows, length), scores, NEG_LARGE)
    row_peak = jnp.max(scores, axis=-1, keepdims=True)
    exp_values = jnp.exp(scores - row_peak)
    exp_total = jnp.sum(exp_values, axis=-1, keepdims=True)
    soft_weights = (exp_values / exp_total).astype(jnp.bfloat16)
    outputs = [
        jnp.einsum(
            "hgqk,hkd->hgqd", soft_weights, value_low, preferred_element_type=jnp.float32
        ).astype(jnp.bfloat16)
    ]
    totals = [row_peak + jnp.log(exp_total)]
    return (jnp.concatenate(outputs, axis=2), jnp.concatenate(totals, axis=2))


def slot_attention_back(query_low, key_low, value_low, totals, heads_gradient, length):
    block_rows = min(512, SLOT_ROWS)
    score_scale = HEAD_SIZE ** (-0.5)
    grad_keys = jnp.zeros(key_low.shape, jnp.float32)
    value_gradients = jnp.zeros(value_low.shape, jnp.float32)
    scores = (
        jnp.einsum("hgqd,hkd->hgqk", query_low, key_low, preferred_element_type=jnp.float32)
        * score_scale
    )
    allowed = key_mask(block_rows, block_rows, length)
    soft_weights = jnp.where(allowed, jnp.exp(scores - totals[:, :, 0:block_rows]), 0.0)
    back_soft = jnp.einsum(
        "hgqd,hkd->hgqk", heads_gradient, value_low, preferred_element_type=jnp.float32
    )
    inner_sums = jnp.sum(soft_weights * back_soft, axis=-1, keepdims=True)
    back_scores = (soft_weights * (back_soft - inner_sums)).astype(jnp.bfloat16)
    query_parts = [
        jnp.einsum("hgqk,hkd->hgqd", back_scores, key_low, preferred_element_type=jnp.float32)
        * score_scale
    ]
    grad_keys = grad_keys.at[:, :block_rows].add(
        jnp.einsum("hgqk,hgqd->hkd", back_scores, query_low, preferred_element_type=jnp.float32)
        * score_scale
    )
    value_gradients = value_gradients.at[:, :block_rows].add(
        jnp.einsum(
            "hgqk,hgqd->hkd",
            soft_weights.astype(jnp.bfloat16),
            heads_gradient,
            preferred_element_type=jnp.float32,
        )
    )
    return (jnp.concatenate(query_parts, axis=2), grad_keys, value_gradients)


def shards(
    tokens,
    cotangent,
    lengths,
    w_in,
    w_out,
    gains,
    first_in,
    first_out,
    gain_first,
    second_in,
    second_out,
    gain_second,
):
    slot_batch = lengths.shape[0]
    row_total = tokens.shape[0]
    query_group_width = QUERY_HEADS // KEY_VALUE_HEADS
    gathered_in, gathered_out, gathered_gains = (
        lax.all_gather(w_in.astype(jnp.bfloat16), "shard", axis=0, tiled=True),
        lax.all_gather(w_out.astype(jnp.bfloat16), "shard", axis=0, tiled=True),
        lax.all_gather(gains.astype(jnp.bfloat16), "shard", axis=0, tiled=True),
    )
    gain_all = gathered_gains.astype(jnp.float32)
    gain_in = gain_all[:MODEL_WIDTH]
    gain_post = gain_all[MODEL_WIDTH : 2 * MODEL_WIDTH]
    gain_query = gain_all[2 * MODEL_WIDTH : 2 * MODEL_WIDTH + HEAD_SIZE]
    gain_key = gain_all[2 * MODEL_WIDTH + HEAD_SIZE :]
    proj_qkv = gathered_in[:, :QKVC]
    proj_mix = gathered_in[:, QKVC:]
    proj_attn = gathered_out[: QUERY_HEADS * HEAD_SIZE]
    proj_down = gathered_out[QUERY_HEADS * HEAD_SIZE :]
    cosine, sine = rope_tables(SLOT_ROWS, HEAD_SIZE)
    layer_inputs = tokens.astype(jnp.float32)
    normed, pull_in = jax.vjp(rms_scale, layer_inputs, gain_in)
    normed_low = normed.astype(jnp.bfloat16)
    unnormed_rows = jnp.dot(normed_low, proj_qkv, preferred_element_type=jnp.float32).reshape(
        slot_batch, SLOT_ROWS, QKVC
    )

    def prep_local(raw_part, gain_q, gain_k):
        return prepare(raw_part, gain_q, gain_k, cosine, sine)

    (queries, key_head_rows, value_head_rows), pull_prep = jax.vjp(
        prep_local, unnormed_rows, gain_query, gain_key
    )
    query_low = (
        queries.astype(jnp.bfloat16)
        .reshape(slot_batch, SLOT_ROWS, KEY_VALUE_HEADS, query_group_width, HEAD_SIZE)
        .transpose(0, 2, 3, 1, 4)
    )
    key_low = key_head_rows.astype(jnp.bfloat16).transpose(0, 2, 1, 3)
    value_low = value_head_rows.astype(jnp.bfloat16).transpose(0, 2, 1, 3)
    attended, totals = lax.map(
        lambda slot_item: slot_attention(slot_item[0], slot_item[1], slot_item[2], slot_item[3]),
        (query_low, key_low, value_low, lengths),
    )
    attended_rows = attended.transpose(0, 3, 1, 2, 4).reshape(row_total, QUERY_HEADS * HEAD_SIZE)
    middle = layer_inputs + jnp.dot(attended_rows, proj_attn, preferred_element_type=jnp.float32)
    normed_post, pull_post = jax.vjp(rms_scale, middle, gain_post)
    post_low = normed_post.astype(jnp.bfloat16)
    mixed = jnp.dot(post_low, proj_mix, preferred_element_type=jnp.float32)
    hidden, pull_gate = jax.vjp(gated_unit, mixed)
    hidden_low = hidden.astype(jnp.bfloat16)
    layer_output = (
        middle + jnp.dot(hidden_low, proj_down, preferred_element_type=jnp.float32)
    ).astype(jnp.bfloat16)
    positions = jnp.arange(SLOT_ROWS, dtype=jnp.int32)
    valid_row_count = (
        (positions[None, :] < lengths[:, None]).astype(jnp.float32).reshape(row_total, 1)
    )
    back_out = cotangent.astype(jnp.float32) * valid_row_count
    back_out_low = back_out.astype(jnp.bfloat16)
    grad_down = outer_sum(hidden_low, back_out_low)
    back_hidden = back_product(back_out_low, proj_down)
    (back_mixed,) = pull_gate(back_hidden)
    mixed_low = back_mixed.astype(jnp.bfloat16)
    grad_mix = outer_sum(post_low, mixed_low)
    back_post = back_product(mixed_low, proj_mix)
    back_middle, grad_gain_post = pull_post(back_post)
    back_middle = back_middle + back_out
    middle_low = back_middle.astype(jnp.bfloat16)
    grad_attn = outer_sum(attended_rows, middle_low)
    attended_gradient = back_product(middle_low, proj_attn).astype(jnp.bfloat16)
    heads_gradient = attended_gradient.reshape(
        slot_batch, SLOT_ROWS, KEY_VALUE_HEADS, query_group_width, HEAD_SIZE
    ).transpose(0, 2, 3, 1, 4)
    grad_query, grad_key, grad_value = lax.map(
        lambda slot_item: slot_attention_back(
            slot_item[0], slot_item[1], slot_item[2], slot_item[3], slot_item[4], slot_item[5]
        ),
        (query_low, key_low, value_low, totals, heads_gradient, lengths),
    )
    grad_query = grad_query.transpose(0, 3, 1, 2, 4).reshape(
        slot_batch, SLOT_ROWS, QUERY_HEADS, HEAD_SIZE
    )
    grad_key = grad_key.transpose(0, 2, 1, 3)
    grad_value = grad_value.transpose(0, 2, 1, 3)
    back_raw, grad_gain_query, grad_gain_key = pull_prep((grad_query, grad_key, grad_value))
    raw_low = back_raw.reshape(row_total, QKVC).astype(jnp.bfloat16)
    grad_qkv = outer_sum(normed_low, raw_low)
    back_normed = back_product(raw_low, proj_qkv)
    back_inputs, grad_gain_in = pull_in(back_normed)
    layer_input_gradient = (back_middle + back_inputs).astype(jnp.bfloat16)
    output_values = layer_output.astype(jnp.float32)
    value_gradients = layer_input_gradient.astype(jnp.float32)
    sum_out, sum_grad, sum_count = lax.psum(
        (
            jnp.sum(valid_row_count * output_values * output_values),
            jnp.sum(valid_row_count * value_gradients * value_gradients),
            jnp.sum(valid_row_count),
        ),
        ("dp", "shard"),
    )
    valid_rms = jnp.sqrt(jnp.stack([sum_out, sum_grad]) / (sum_count * MODEL_WIDTH))
    owners = lax.axis_size("shard")
    grad_in = jnp.concatenate([grad_qkv, grad_mix], axis=1)
    grad_out = jnp.concatenate([grad_attn, grad_down], axis=0)
    grad_gain = jnp.concatenate(
        [grad_gain_in, grad_gain_post, grad_gain_query, grad_gain_key]
    ).reshape(owners, GN // owners)
    part_in, part_out, part_gain = (
        lax.psum_scatter(grad_in, "dp", scatter_dimension=1, tiled=True),
        lax.psum_scatter(grad_out, "dp", scatter_dimension=1, tiled=True),
        lax.psum_scatter(grad_gain, "dp", scatter_dimension=1, tiled=True),
    )
    owned_in, owned_out, owned_gain = (
        lax.psum_scatter(part_in, "shard", scatter_dimension=0, tiled=True),
        lax.psum_scatter(part_out, "shard", scatter_dimension=0, tiled=True),
        lax.psum_scatter(part_gain, "shard", scatter_dimension=0, tiled=True),
    )
    summed_in, summed_out, summed_gain = (
        lax.all_gather(owned_in, "dp", axis=1, tiled=True),
        lax.all_gather(owned_out, "dp", axis=1, tiled=True),
        lax.all_gather(owned_gain, "dp", axis=1, tiled=True),
    )
    summed_gain = summed_gain.reshape(-1)
    new_w_in, new_first_in, new_second_in = adamw_update(
        w_in, first_in, second_in, summed_in, MATRIX_RATE, MATRIX_DECAY
    )
    new_w_out, new_first_out, new_second_out = adamw_update(
        w_out, first_out, second_out, summed_out, MATRIX_RATE, MATRIX_DECAY
    )
    new_gains, new_gain_first, new_gain_second = adamw_update(
        gains, gain_first, gain_second, summed_gain, GAIN_RATE, 0.0
    )
    return (
        layer_output,
        layer_input_gradient,
        new_w_in,
        new_w_out,
        new_gains,
        new_first_in,
        new_first_out,
        new_gain_first,
        new_second_in,
        new_second_out,
        new_gain_second,
        valid_rms,
    )


def low(values):
    return values.astype(jnp.bfloat16)


def wide(values):
    return values.astype(jnp.float32)


def mul(left, right):
    return jnp.dot(left, right, preferred_element_type=jnp.float32)


def mul_bt(left, right):
    return lax.dot_general(
        left, right, (((1,), (1,)), ((), ())), preferred_element_type=jnp.float32
    )


def mul_at(left, right):
    return lax.dot_general(
        left, right, (((0,), (0,)), ((), ())), preferred_element_type=jnp.float32
    )


def whole(shape):
    return pl.BlockSpec(shape, lambda *_: (0,) * len(shape))


def resident(shape, index=None):
    index = index or (0,) * len(shape)
    return pl.BlockSpec(shape, lambda *_: index, pipeline_mode=pl.Buffered(1))


def shape_of(shape, kind):
    return jax.ShapeDtypeStruct(shape, kind)


GAIN_IN = slice(0, MODEL_WIDTH)
GAIN_POST = slice(MODEL_WIDTH, 2 * MODEL_WIDTH)
GAIN_Q = slice(2 * MODEL_WIDTH, 2 * MODEL_WIDTH + HEAD_SIZE)
GAIN_K = slice(2 * MODEL_WIDTH + HEAD_SIZE, GN)
BF = jnp.bfloat16
F32 = jnp.float32
VMEM_BYTES = 64 * 1024 * 1024


def params(axes=1, limit=VMEM_BYTES):
    return pltpu.CompilerParams(
        dimension_semantics=("arbitrary",) * axes, vmem_limit_bytes=limit
    )


def split_columns(values, core):
    half = values.shape[1] // 2
    first, second = values[:, :half], values[:, half:]
    mine = core == 0
    return jnp.where(mine, first, second), jnp.where(mine, second, first)


def join_columns(own, other, core):
    mine = core == 0
    return jnp.concatenate(
        [jnp.where(mine, own, other), jnp.where(mine, other, own)], axis=1
    )


def cast_qkv_kernel(q_ref, k_ref, v_ref, out_ref):
    for at in range(out_ref.shape[0]):
        out_ref[at, :, :256] = low(q_ref[:, at * 256 : at * 256 + 256])
        out_ref[at, :, 256:384] = low(k_ref[:, at * 128 : at * 128 + 128])
        out_ref[at, :, 384:] = low(v_ref[:, at * 128 : at * 128 + 128])


def cast_qkv(w_in):
    rows = w_in.shape[0]
    width = 256
    return pl.pallas_call(
        cast_qkv_kernel,
        grid=(KEY_VALUE_HEADS * 128 // width,),
        in_specs=[
            pl.BlockSpec((rows, 2 * width), lambda g: (0, g)),
            pl.BlockSpec((rows, width), lambda g: (0, 2048 // width + g)),
            pl.BlockSpec((rows, width), lambda g: (0, 3072 // width + g)),
        ],
        out_specs=pl.BlockSpec((width // 128, rows, 512), lambda g: (g, 0, 0)),
        out_shape=shape_of((KEY_VALUE_HEADS, rows, 512), BF),
        compiler_params=params(),
        name="cast_qkv",
    )(w_in, w_in, w_in)


def cast_rows_kernel(in_ref, out_ref):
    out_ref[...] = low(in_ref[...])


def cast_rows(values, block):
    rows, columns = values.shape
    spec = pl.BlockSpec((block, columns), lambda i: (i, 0))
    return pl.pallas_call(
        cast_rows_kernel,
        grid=(rows // block,),
        in_specs=[spec],
        out_specs=spec,
        out_shape=shape_of(values.shape, BF),
        compiler_params=params(),
        name="cast_out",
    )(values)


def cast_mix_kernel(gate_ref, up_ref, *out_refs):
    half = gate_ref.shape[0] // 2
    for at, out_ref in enumerate(out_refs):
        rows = slice(at * half, at * half + half)
        out_ref[0, :, :FFB] = low(gate_ref[rows, :])
        out_ref[0, :, FFB:] = low(up_ref[rows, :])


FFB = 1024
FF_STEPS = FF // FFB


def cast_mix(w_in):
    rows = w_in.shape[0]
    return pl.pallas_call(
        cast_mix_kernel,
        grid=(FF_STEPS,),
        in_specs=[
            pl.BlockSpec((rows, FFB), lambda j: (0, QKVC // FFB + j)),
            pl.BlockSpec((rows, FFB), lambda j: (0, (QKVC + FF) // FFB + j)),
        ],
        out_specs=[pl.BlockSpec((1, rows // 2, 2 * FFB), lambda j: (j, 0, 0))] * 2,
        out_shape=[shape_of((FF_STEPS, rows // 2, 2 * FFB), BF)] * 2,
        compiler_params=params(),
        name="cast_mix",
    )(w_in, w_in)


def turn(values):
    return pltpu.roll(values, HEAD_SIZE // 2, 1)


def head_norm(raw):
    scale = lax.rsqrt(jnp.mean(raw * raw, axis=-1, keepdims=True) + EPSILON)
    return raw * scale, scale


def block_mask(first_row, rows, keys, length):
    row = first_row + lax.broadcasted_iota(jnp.int32, (2 * rows, keys), 0) % rows
    key = lax.broadcasted_iota(jnp.int32, (2 * rows, keys), 1)
    return (key <= row) & (key < length)


def both_heads(values):
    return jnp.concatenate([values[:, :128], values[:, 128:]], axis=0)


QB = 128


def forward_kernel(
    meta_ref,
    x_ref,
    gain_ref,
    cos_ref,
    sin_ref,
    own_ref,
    other_ref,
    o_ref,
    qkv_ref,
    u_ref,
    lse_ref,
    a_own_ref,
    a_other_ref,
):
    core, length = meta_ref[0], meta_ref[1]

    @pl.when(pl.program_id(0) == 0)
    def _():
        x = wide(x_ref[...])
        scale = lax.rsqrt(jnp.mean(x * x, axis=-1, keepdims=True) + EPSILON)
        own, other = split_columns(low(x * scale * gain_ref[:, GAIN_IN]), core)
        a_own_ref[...] = own
        a_other_ref[...] = other

    u = mul(a_own_ref[...], own_ref[0]) + mul(a_other_ref[...], other_ref[0])
    u_ref[0] = u[:, :384]
    cosine, sine = cos_ref[...], sin_ref[...]
    gain_q, gain_k = gain_ref[:, GAIN_Q], gain_ref[:, GAIN_K]
    for part in range(3):
        normed, _ = head_norm(u[:, part * 128 : part * 128 + 128])
        normed = normed * (gain_k if part == 2 else gain_q)
        qkv_ref[0, :, part * 128 : part * 128 + 128] = low(
            normed * cosine + turn(normed) * sine
        )
    qkv_ref[0, :, 384:] = low(u[:, 384:])
    score_scale = HEAD_SIZE ** (-0.5)
    for first in range(0, SLOT_ROWS, QB):
        keys = first + QB
        rows = slice(first, first + QB)
        k = qkv_ref[0, :keys, 256:384]
        v = qkv_ref[0, :keys, 384:]
        scores = mul_bt(both_heads(qkv_ref[0, rows, :256]), k) * score_scale
        scores = jnp.where(block_mask(first, QB, keys, length), scores, NEG_LARGE)
        peak = jnp.max(scores, axis=-1, keepdims=True)
        powers = jnp.exp(scores - peak)
        total = jnp.sum(powers, axis=-1, keepdims=True)
        o = low(mul(low(powers * (1.0 / total)), v))
        level = peak + jnp.log(total)
        for head in range(2):
            half = slice(head * QB, head * QB + QB)
            columns = slice(head * 128, head * 128 + 128)
            o_ref[rows, columns] = o[half]
            lse_ref[0, rows, columns] = jnp.broadcast_to(level[half], (QB, 128))


def forward(meta, tokens, gains, cosine, sine, own, other):
    rows = SLOT_ROWS
    half = MODEL_WIDTH // 2
    return pl.pallas_call(
        forward_kernel,
        grid_spec=pltpu.PrefetchScalarGridSpec(
            num_scalar_prefetch=1,
            grid=(KEY_VALUE_HEADS,),
            in_specs=[
                resident((rows, MODEL_WIDTH)),
                resident((1, GN)),
                resident((rows, HEAD_SIZE)),
                resident((rows, HEAD_SIZE)),
                pl.BlockSpec((1, half, 512), lambda g, _: (g, 0, 0)),
                pl.BlockSpec((1, half, 512), lambda g, _: (g, 0, 0)),
            ],
            out_specs=[
                pl.BlockSpec((rows, 256), lambda g, _: (0, g)),
                pl.BlockSpec((1, rows, 512), lambda g, _: (g, 0, 0)),
                pl.BlockSpec((1, rows, 384), lambda g, _: (g, 0, 0)),
                pl.BlockSpec((1, rows, 256), lambda g, _: (g, 0, 0)),
                whole((rows, half)),
                whole((rows, half)),
            ],
        ),
        out_shape=[
            shape_of((rows, QUERY_HEADS * HEAD_SIZE), BF),
            shape_of((KEY_VALUE_HEADS, rows, 512), BF),
            shape_of((KEY_VALUE_HEADS, rows, 384), F32),
            shape_of((KEY_VALUE_HEADS, rows, 256), F32),
            shape_of((rows, half), BF),
            shape_of((rows, half), BF),
        ],
        compiler_params=params(),
        name="forward",
    )(meta, tokens, gains, cosine, sine, own, other)


def unit_kernel(
    meta_ref,
    o_ref,
    x_ref,
    e_ref,
    gain_ref,
    wo_ref,
    wd_ref,
    own_top_ref,
    own_end_ref,
    other_top_ref,
    other_end_ref,
    y_ref,
    dgate_ref,
    dup_ref,
    b_own_ref,
    b_other_ref,
    left_ref,
    send_ref,
    dmid_ref,
    dlow_ref,
    small_ref,
    mid_s,
    y_s,
    db_own_s,
    db_other_s,
):
    core, length = meta_ref[0], meta_ref[1]
    step = pl.program_id(0)
    quarter = own_top_ref.shape[1]
    weights = [
        (b_own_ref, slice(0, quarter), db_own_s, own_top_ref),
        (b_own_ref, slice(quarter, None), db_own_s, own_end_ref),
        (b_other_ref, slice(0, quarter), db_other_s, other_top_ref),
        (b_other_ref, slice(quarter, None), db_other_s, other_end_ref),
    ]
    attended = QUERY_HEADS * HEAD_SIZE
    valid = lax.broadcasted_iota(jnp.int32, (SLOT_ROWS, 1), 0) < length

    @pl.when(step == 0)
    def _():
        middle = wide(x_ref[...]) + mul(o_ref[...], wo_ref[...])
        mid_s[...] = middle
        y_s[...] = middle
        scale = lax.rsqrt(jnp.mean(middle * middle, axis=-1, keepdims=True) + EPSILON)
        own, other = split_columns(low(middle * scale * gain_ref[:, GAIN_POST]), core)
        b_own_ref[...] = own
        b_other_ref[...] = other
        db_own_s[...] = jnp.zeros_like(db_own_s)
        db_other_s[...] = jnp.zeros_like(db_other_s)

        @pl.when(core == 0)
        def _():
            left_ref[:, :attended] = o_ref[...]

        @pl.when(core != 0)
        def _():
            send_ref[:, :attended] = o_ref[...]

    e = e_ref[...]
    for part in range(FFB // 512):
        gates = slice(part * 512, part * 512 + 512)
        ups = slice(FFB + part * 512, FFB + part * 512 + 512)
        gate = sum(mul(b_ref[:, rows], w_ref[0, :, gates]) for b_ref, rows, _, w_ref in weights)
        up = sum(mul(b_ref[:, rows], w_ref[0, :, ups]) for b_ref, rows, _, w_ref in weights)
        down = wd_ref[gates, :]
        dh = mul_bt(e, down)
        sigma = 1.0 / (1.0 + jnp.exp(-gate))
        silu = gate * sigma
        hidden = low(silu * up)
        dgate = low(dh * up * (sigma * (1.0 + gate * (1.0 - sigma))))
        dup = low(dh * silu)
        y_s[...] += mul(hidden, down)
        for _, rows, db_s, w_ref in weights:
            db_s[:, rows] += mul_bt(dgate, w_ref[0, :, gates]) + mul_bt(dup, w_ref[0, :, ups])
        dgate_ref[:, gates] = dgate
        dup_ref[:, gates] = dup

        place = pl.multiple_of(jnp.maximum(step * FFB + part * 512 - 512, 0), 512)
        first_rows = (step == 0) & (part == 0)

        @pl.when(first_rows & (core == 0))
        def _():
            left_ref[:, attended:] = hidden

        @pl.when(first_rows & (core != 0))
        def _():
            send_ref[:, attended : attended + 512] = hidden

        @pl.when(jnp.logical_not(first_rows) & (core == 0))
        def _():
            send_ref[:, pl.ds(place, 512)] = hidden

        @pl.when(jnp.logical_not(first_rows) & (core != 0))
        def _():
            left_ref[:, pl.ds(place, 512)] = hidden

    @pl.when(step == FF_STEPS - 1)
    def _():
        y = low(y_s[...])
        y_ref[...] = y
        y = wide(y)
        total = jnp.sum(jnp.where(valid, y * y, 0.0))
        db = join_columns(db_own_s[...], db_other_s[...], core)
        middle = mid_s[...]
        scale = lax.rsqrt(jnp.mean(middle * middle, axis=-1, keepdims=True) + EPSILON)
        normed = middle * scale
        dn = db * gain_ref[:, GAIN_POST]
        dmid = wide(e) + scale * (
            dn - normed * jnp.mean(dn * normed, axis=-1, keepdims=True)
        )
        dmid_ref[...] = dmid
        dlow = low(dmid)
        dlow_ref[...] = dlow
        send_ref[:, left_ref.shape[1] :] = dlow
        small_ref[0:1, :] = jnp.sum(db * normed, axis=0, keepdims=True)
        small_ref[1:8, :] = jnp.full((7, MODEL_WIDTH), total)


def unit(meta, o, tokens, e, gains, w_out, *mix):
    rows = SLOT_ROWS
    half = MODEL_WIDTH // 2
    attended = QUERY_HEADS * HEAD_SIZE
    owned = w_out.shape[0] // 2
    return pl.pallas_call(
        unit_kernel,
        grid_spec=pltpu.PrefetchScalarGridSpec(
            num_scalar_prefetch=1,
            grid=(FF_STEPS,),
            in_specs=[
                resident((rows, attended)),
                resident((rows, MODEL_WIDTH)),
                resident((rows, MODEL_WIDTH)),
                resident((1, GN)),
                resident((attended, MODEL_WIDTH)),
                pl.BlockSpec((FFB, MODEL_WIDTH), lambda j, _: (attended // FFB + j, 0)),
            ]
            + [pl.BlockSpec((1, half // 2, 2 * FFB), lambda j, _: (j, 0, 0))] * 4,
            out_specs=[
                whole((rows, MODEL_WIDTH)),
                pl.BlockSpec((rows, FFB), lambda j, _: (0, j)),
                pl.BlockSpec((rows, FFB), lambda j, _: (0, j)),
                whole((rows, half)),
                whole((rows, half)),
                whole((rows, owned)),
                whole((rows, owned + MODEL_WIDTH)),
                whole((rows, MODEL_WIDTH)),
                whole((rows, MODEL_WIDTH)),
                whole((8, MODEL_WIDTH)),
            ],
            scratch_shapes=[
                pltpu.VMEM((rows, MODEL_WIDTH), F32),
                pltpu.VMEM((rows, MODEL_WIDTH), F32),
                pltpu.VMEM((rows, half), F32),
                pltpu.VMEM((rows, half), F32),
            ],
        ),
        out_shape=[
            shape_of((rows, MODEL_WIDTH), BF),
            shape_of((rows, FF), BF),
            shape_of((rows, FF), BF),
            shape_of((rows, half), BF),
            shape_of((rows, half), BF),
            shape_of((rows, owned), BF),
            shape_of((rows, owned + MODEL_WIDTH), BF),
            shape_of((rows, MODEL_WIDTH), F32),
            shape_of((rows, MODEL_WIDTH), BF),
            shape_of((8, MODEL_WIDTH), F32),
        ],
        compiler_params=params(),
        name="unit",
    )(meta, o, tokens, e, gains, w_out, w_out, *mix)


def backward_kernel(
    meta_ref,
    dmid_ref,
    dlow_ref,
    x_ref,
    gain_ref,
    cos_ref,
    sin_ref,
    wo_ref,
    own_ref,
    other_ref,
    qkv_ref,
    u_ref,
    lse_ref,
    small_in_ref,
    dx_ref,
    duq_first_ref,
    duq_last_ref,
    duk_ref,
    duv_ref,
    small_ref,
    da_own_s,
    da_other_s,
    head_s,
    dk_s,
    dv_s,
):
    core, length = meta_ref[0], meta_ref[1]
    step = pl.program_id(0)

    @pl.when(step == 0)
    def _():
        for sums in (da_own_s, da_other_s, head_s):
            sums[...] = jnp.zeros_like(sums)

    cosine, sine = cos_ref[...], sin_ref[...]
    score_scale = HEAD_SIZE ** (-0.5)
    do = low(mul_bt(dlow_ref[...], wo_ref[...]))

    def through(grad, raw, gain, slot):
        back = grad * cosine - turn(grad) * sine
        normed, scale = head_norm(raw)
        head_s[slot : slot + 1, :] += jnp.sum(back * normed, axis=0, keepdims=True)
        dn = back * gain
        return low(scale * (dn - normed * jnp.mean(dn * normed, axis=-1, keepdims=True)))

    grad_rows = []
    for first in reversed(range(0, SLOT_ROWS, QB)):
        keys = first + QB
        rows = slice(first, first + QB)
        q = both_heads(qkv_ref[0, rows, :256])
        k = qkv_ref[0, :keys, 256:384]
        v = qkv_ref[0, :keys, 384:]
        dos = both_heads(do[rows, :])
        level = jnp.concatenate([lse_ref[0, rows, 0:1], lse_ref[0, rows, 128:129]], axis=0)
        soft = jnp.where(
            block_mask(first, QB, keys, length),
            jnp.exp(mul_bt(q, k) * score_scale - level),
            0.0,
        )
        dsoft = mul_bt(dos, v)
        inner = jnp.sum(soft * dsoft, axis=-1, keepdims=True)
        ds = low(soft * (dsoft - inner))
        grad_rows.insert(0, mul(ds, k))
        grad_k = mul_at(ds, q)
        grad_v = mul_at(low(soft), dos)
        if keys == SLOT_ROWS:
            dk_s[...] = grad_k
            dv_s[...] = grad_v
        else:
            dk_s[:keys, :] += grad_k
            dv_s[:keys, :] += grad_v
    parts = []
    for head in range(2):
        columns = slice(head * 128, head * 128 + 128)
        grad_q = jnp.concatenate([g[head * QB : head * QB + QB] for g in grad_rows], axis=0)
        parts.append(
            through(grad_q * score_scale, u_ref[0, :, columns], gain_ref[:, GAIN_Q], 0)
        )
    parts.append(
        through(dk_s[...] * score_scale, u_ref[0, :, 256:384], gain_ref[:, GAIN_K], 1)
    )
    parts.append(low(dv_s[...]))
    du = jnp.concatenate(parts, axis=1)
    duk_ref[...] = du[:, 256:384]
    duv_ref[...] = du[:, 384:]

    @pl.when(step < KEY_VALUE_HEADS // 2)
    def _():
        duq_first_ref[...] = du[:, :256]

    @pl.when(step >= KEY_VALUE_HEADS // 2)
    def _():
        duq_last_ref[...] = du[:, :256]

    da_own_s[...] += mul_bt(du, own_ref[0])
    da_other_s[...] += mul_bt(du, other_ref[0])

    @pl.when(step == KEY_VALUE_HEADS - 1)
    def _():
        da = join_columns(da_own_s[...], da_other_s[...], core)
        x = wide(x_ref[...])
        scale = lax.rsqrt(jnp.mean(x * x, axis=-1, keepdims=True) + EPSILON)
        normed = x * scale
        dn = da * gain_ref[:, GAIN_IN]
        dx = low(
            dmid_ref[...]
            + scale * (dn - normed * jnp.mean(dn * normed, axis=-1, keepdims=True))
        )
        dx_ref[...] = dx
        dx = wide(dx)
        valid = lax.broadcasted_iota(jnp.int32, (SLOT_ROWS, 1), 0) < length
        total = jnp.sum(jnp.where(valid, dx * dx, 0.0))
        small_ref[0:1, :] = jnp.sum(da * normed, axis=0, keepdims=True)
        small_ref[1:2, :] = small_in_ref[0:1, :]
        small_ref[2:8, :] = jnp.full((6, MODEL_WIDTH), total)
        small_ref[2:3, 0:128] = head_s[0:1, :]
        small_ref[2:3, 128:256] = head_s[1:2, :]
        small_ref[3:4, :] = small_in_ref[1:2, :]
        small_ref[4:5, :] = jnp.full((1, MODEL_WIDTH), 1.0) * length.astype(F32)


def backward(
    meta,
    dmid,
    dlow,
    tokens,
    gains,
    cosine,
    sine,
    w_out,
    own,
    other,
    qkv,
    u,
    lse,
    small,
):
    rows = SLOT_ROWS
    half = MODEL_WIDTH // 2
    middle = KEY_VALUE_HEADS // 2
    return pl.pallas_call(
        backward_kernel,
        grid_spec=pltpu.PrefetchScalarGridSpec(
            num_scalar_prefetch=1,
            grid=(KEY_VALUE_HEADS,),
            in_specs=[
                resident((rows, MODEL_WIDTH)),
                resident((rows, MODEL_WIDTH)),
                resident((rows, MODEL_WIDTH)),
                resident((1, GN)),
                resident((rows, HEAD_SIZE)),
                resident((rows, HEAD_SIZE)),
                pl.BlockSpec((256, MODEL_WIDTH), lambda g, _: (g, 0)),
                pl.BlockSpec((1, half, 512), lambda g, _: (g, 0, 0)),
                pl.BlockSpec((1, half, 512), lambda g, _: (g, 0, 0)),
                pl.BlockSpec((1, rows, 512), lambda g, _: (g, 0, 0)),
                pl.BlockSpec((1, rows, 384), lambda g, _: (g, 0, 0)),
                pl.BlockSpec((1, rows, 256), lambda g, _: (g, 0, 0)),
                resident((8, MODEL_WIDTH)),
            ],
            out_specs=[
                whole((rows, MODEL_WIDTH)),
                pl.BlockSpec((rows, 256), lambda g, _: (0, jnp.minimum(g, middle - 1))),
                pl.BlockSpec((rows, 256), lambda g, _: (0, jnp.maximum(g - middle, 0))),
                pl.BlockSpec((rows, 128), lambda g, _: (0, g)),
                pl.BlockSpec((rows, 128), lambda g, _: (0, g)),
                whole((8, MODEL_WIDTH)),
            ],
            scratch_shapes=[
                pltpu.VMEM((rows, half), F32),
                pltpu.VMEM((rows, half), F32),
                pltpu.VMEM((8, HEAD_SIZE), F32),
                pltpu.VMEM((rows, HEAD_SIZE), F32),
                pltpu.VMEM((rows, HEAD_SIZE), F32),
            ],
        ),
        out_shape=[shape_of((rows, MODEL_WIDTH), BF)]
        + [shape_of((rows, 1024), BF)] * 4
        + [shape_of((8, MODEL_WIDTH), F32)],
        compiler_params=params(),
        name="backward",
    )(meta, dmid, dlow, tokens, gains, cosine, sine, w_out, own, other, qkv, u, lse, small)


def store_pieces(acc, rank, pieces, targets):
    piece = acc.shape[0] // pieces
    share = pieces // len(targets)
    for at in range(pieces):
        source = pl.multiple_of(lax.bitwise_xor(at, rank) * piece, piece)
        place = at % share
        targets[at // share][place * piece : (place + 1) * piece, :] = low(
            acc[pl.ds(source, piece), :]
        )


def quarters(rows, columns):
    return [shape_of((rows // 4, columns), BF)] * 4


def grad_in_kernel(meta_ref, *refs, route, lefts, spans):
    sources, (*targets, acc) = refs[: 2 * (lefts + len(spans))], refs[2 * (lefts + len(spans)) :]
    step = pl.program_id(0)
    for at, (left, start, stop, _) in enumerate(spans):
        l_own, l_got = sources[2 * left : 2 * left + 2]
        r_own, r_got = sources[2 * (lefts + at) : 2 * (lefts + at) + 2]

        @pl.when((step >= start) & (step < stop))
        def _():
            acc[...] = mul_at(l_own[...], r_own[...]) + mul_at(l_got[...], r_got[...])

    store_pieces(acc, meta_ref[route.slot], route.pieces, targets)


def grad_in(meta, lefts, rights, route, block=1024):
    tokens, rows = lefts[0][0].shape
    spans, count = [], 0
    for left, _, _, first, blocks in rights:
        spans.append((left, count, count + blocks, first))
        count += blocks
    outs = quarters(rows, count * block)
    out = pl.BlockSpec((outs[0].shape[0], block), lambda j, _: (0, j))

    def right_spec(start, stop, first):
        return pl.BlockSpec(
            (tokens, block), lambda j, _: (0, first + jnp.clip(j, start, stop - 1) - start)
        )

    return pl.pallas_call(
        functools.partial(grad_in_kernel, route=route, lefts=len(lefts), spans=spans),
        grid_spec=pltpu.PrefetchScalarGridSpec(
            num_scalar_prefetch=1,
            grid=(count,),
            in_specs=[resident((tokens, rows))] * (2 * len(lefts))
            + [right_spec(*span[1:]) for span in spans for _ in range(2)],
            out_specs=[out] * len(outs),
            scratch_shapes=[pltpu.VMEM((rows, block), F32)],
        ),
        out_shape=outs,
        compiler_params=params(),
        name="grad_in",
    )(meta, *(v for left in lefts for v in left), *(v for right in rights for v in right[1:3]))


def grad_out_kernel(
    meta_ref, l_own, l_got, d_own, d_got, e_own, e_got, *targets, route
):
    *targets, acc = targets
    attended = QUERY_HEADS * HEAD_SIZE
    acc[attended:, :] = mul_at(l_own[:, attended:], e_own[...]) + mul_at(
        l_got[:, attended:], e_got[...]
    )

    def upper(own, got):
        for at in range(0, attended, 512):
            rows = slice(at, at + 512)
            acc[rows, :] = mul_at(l_own[:, rows], own) + mul_at(l_got[:, rows], got)

    @pl.when(meta_ref[0] == 0)
    def _():
        upper(d_own[...], d_got[...])

    @pl.when(meta_ref[0] != 0)
    def _():
        upper(e_own[...], e_got[...])

    store_pieces(acc, meta_ref[route.slot], route.pieces, targets)


def grad_out(meta, l_own, got, d_own, e_own, e_got, route):
    tokens, rows = l_own.shape
    block = 512
    outs = quarters(rows, MODEL_WIDTH)
    left = resident((tokens, rows))
    right = pl.BlockSpec((tokens, block), lambda j, _: (0, j))
    out = pl.BlockSpec((outs[0].shape[0], block), lambda j, _: (0, j))
    return pl.pallas_call(
        functools.partial(grad_out_kernel, route=route),
        grid_spec=pltpu.PrefetchScalarGridSpec(
            num_scalar_prefetch=1,
            grid=(MODEL_WIDTH // block,),
            in_specs=[
                left,
                left,
                right,
                pl.BlockSpec((tokens, block), lambda j, _: (0, rows // block + j)),
                right,
                right,
            ],
            out_specs=[out] * len(outs),
            scratch_shapes=[pltpu.VMEM((rows, block), F32)],
        ),
        out_shape=outs,
        compiler_params=params(),
        name="grad_out",
    )(meta, l_own, got, d_own, got, e_own, e_got)


class Route:
    def __init__(self, slot, bits, chips, cores):
        self.slot, self.chips, self.cores = slot, chips, cores
        even = list(bits)
        crossed = {0: 1, 1: 0}
        self.orders = [even, [crossed.get(bit, bit) for bit in even]]
        self.stages = len(even)
        self.pieces = 1 << self.stages
        self.groups = {}
        for chip in range(chips):
            for core in range(cores):
                kept = sum(1 << bit for bit in self.orders[core % 2])
                self.groups.setdefault((core, chip & kept), []).append(chip * cores + core)
        self.groups = list(self.groups.values())
        self.whole = len(self.groups) == chips * cores

    def rank(self, chip, core):
        def code(order):
            value = 0
            for bit in order:
                value = 2 * value + ((chip >> bit) & 1)
            return value

        return jnp.where(core % 2 == 0, code(self.orders[0]), code(self.orders[1]))

    def swap(self, values, stage):
        pairs = [
            (
                chip * self.cores + core,
                (chip ^ (1 << self.orders[core % 2][stage])) * self.cores + core,
            )
            for chip in range(self.chips)
            for core in range(self.cores)
        ]
        return lax.ppermute(values, ("dp", "shard"), pairs)


class Line:
    def __init__(self):
        self.last = None

    def __call__(self, operation, *operands):
        if self.last is not None:
            operands = lax.optimization_barrier((*operands, self.last))[:-1]
        result = operation(*operands)
        self.last = result[0] if isinstance(result, (tuple, list)) else result
        return result


class Sum:
    def __init__(self, line, route, name):
        self.line, self.route, self.name = line, route, name

    def swap(self, values, stage, what):
        with jax.named_scope(f"{self.name}_{what}_{stage}"):
            return self.route.swap(values, stage)

    def begin(self, operation, *operands):
        *self.keeps, send, first = self.line(operation, *operands)
        self.first_got = self.swap(first, 0, "halving_first")
        self.got = self.swap(send, 0, "halving")
        self.stage = 0

    def add_sent(self):
        send = self.line(lambda a, b: low(wide(a) + wide(b)), self.keeps[1], self.first_got)
        self.next_got = self.swap(send, 1, "halving")

    def add_kept(self):
        self.keep = self.line(lambda a, b: low(wide(a) + wide(b)), self.keeps[0], self.got)
        self.got, self.stage = self.next_got, 1

    def add(self):
        half = self.keep.shape[0] // 2
        if self.stage == self.route.stages - 1:
            self.mine = self.line(lambda a, b: low(wide(a) + wide(b)), self.keep, self.got)
            if self.route.whole:
                self.got = self.swap(self.mine, self.stage, "doubling")
            else:
                with jax.named_scope(f"{self.name}_rest"):
                    self.mine = lax.psum(
                        self.mine, ("dp", "shard"), axis_index_groups=self.route.groups
                    )
            return
        send = self.line(lambda a, b: low(wide(a[half:]) + wide(b[half:])), self.keep, self.got)
        self.stage += 1
        got = self.swap(send, self.stage, "halving")
        self.keep = self.line(lambda a, b: low(wide(a[:half]) + wide(b[:half])), self.keep, self.got)
        self.got = got

    def back(self):
        self.mine = lax.optimization_barrier((self.mine, self.line.last))[0]
        self.got = self.swap(self.mine, 1, "doubling")
        self.far = [self.swap(self.mine, 0, "doubling")]

    def join(self):
        if self.stage > 1:
            self.mine = self.line(
                lambda a, b: jnp.concatenate([a, b], axis=0), self.mine, self.got
            )
            self.stage -= 1
            self.got = self.swap(self.mine, self.stage, "doubling")
            if self.stage == 1:
                self.far = [self.swap(self.mine, 0, "doubling")]
        else:
            self.got = lax.optimization_barrier((self.got, self.line.last))[0]
            self.far.append(self.swap(self.got, 0, "doubling_last"))
            self.near = [self.mine, self.got]


def adam(weight, first, second, gradient, rate, decay):
    first = BETA_ONE * first + (1.0 - BETA_ONE) * gradient
    second = BETA_TWO * second + ((1.0 - BETA_TWO) * gradient) * gradient
    square = second * (1.0 / (1.0 - BETA_TWO**STEP))
    root = square * lax.rsqrt(square) + ADAM_EPSILON
    step = (first * (rate / (1.0 - BETA_ONE**STEP))) / root
    return weight * (1.0 - rate * decay) - step, first, second


def adam_kernel(meta_ref, *refs, route, joint, parts):
    pairs = [refs[2 * at : 2 * at + 2] for at in range(parts)]
    w_ref, f_ref, s_ref = refs[2 * parts : 2 * parts + 3]
    new_w, new_f, new_s = refs[-3:]
    pieces = route.pieces // 2 if joint else route.pieces // 4
    piece = w_ref.shape[0] // pieces
    inner = lax.rem(meta_ref[route.slot], pieces)
    share = route.pieces // 4

    def update(*g_refs):
        for at in range(pieces):
            source = pl.multiple_of(lax.bitwise_xor(at, inner) % share * piece, piece)
            there = slice(at * piece, (at + 1) * piece)
            new_w[there, :], new_f[there, :], new_s[there, :] = adam(
                w_ref[there, :],
                f_ref[there, :],
                s_ref[there, :],
                wide(g_refs[at // share][pl.ds(source, piece), :]),
                MATRIX_RATE,
                MATRIX_DECAY,
            )

    step = pl.program_id(0)
    for at, (near, far) in enumerate(pairs):
        now = (step if joint else step // 2) == at
        near_first = inner < share if joint else step % 2 == 0

        @pl.when(now & near_first)
        def _():
            update(near, far)

        @pl.when(now & jnp.logical_not(near_first))
        def _():
            update(far, near)


def adam_call(meta, route, gradients, states, done, block, place, part, joint):
    rows, columns = gradients[0].shape
    parts = len(gradients) // 2
    steps = 1 if joint else 2
    tall = rows * 2 // steps
    last = columns // block - 1

    def g_spec(at):
        first = at // 2 if joint else at
        return pl.BlockSpec(
            (rows, block),
            lambda t, j, m: (0, jnp.where(t == first, j, jnp.where(t < first, 0, last))),
        )

    spec = pl.BlockSpec(
        (tall, block),
        lambda t, j, m: (
            lax.bitwise_xor(t + part * steps, m[route.slot] // (route.pieces // (2 * steps))),
            place(j),
        ),
    )
    return pl.pallas_call(
        functools.partial(adam_kernel, route=route, joint=joint, parts=parts),
        grid_spec=pltpu.PrefetchScalarGridSpec(
            num_scalar_prefetch=1,
            grid=(parts * steps, columns // block),
            in_specs=[g_spec(at) for at in range(2 * parts)]
            + [spec, spec, spec]
            + [pl.BlockSpec(memory_space=pl.ANY)] * len(done),
            out_specs=[spec, spec, spec],
        ),
        out_shape=[shape_of(states[0].shape, F32)] * 3,
        input_output_aliases={4 + 2 * parts + i: i for i in range(len(done))},
        compiler_params=params(2),
        name="adam",
    )(meta, *gradients, *states, *done)


def rope_constants():
    index = np.arange(HEAD_SIZE // 2, dtype=np.float32)
    frequency = np.exp(index * np.float32(-2.0 * math.log(1000000.0) / HEAD_SIZE))
    angles = np.arange(SLOT_ROWS, dtype=np.float32)[:, None] * frequency[None, :]
    cosine, sine = np.cos(angles), np.sin(angles)
    return (
        np.concatenate([cosine, cosine], axis=1).astype(np.float32),
        np.concatenate([-sine, sine], axis=1).astype(np.float32),
    )


def core_swap(values):
    return lax.ppermute(values, "shard", [(0, 1), (1, 0)])


SUM_ROUTES = (0, 1, 3)

SCHEDULE = (
    "out", "mix", "out>", "K", "small", "mix>", "out*", "mix*", "out+", "mix+", "qkv",
    "out+", "mix+", "qkv>", "mix+", "out+", "mix=", "qkv*", "out=", "small+", "qkv+",
    "small+", "mix=", "out=", "small+", "mix=", "mix!0", "small+", "out=", "out!0", "qkv-",
    "mix!1", "out!1", "qkv=", "qkv!0", "small+", "qkv!1",
)


def slot_shards(
    tokens,
    cotangent,
    lengths,
    w_in,
    w_out,
    gains,
    first_in,
    first_out,
    gain_first,
    second_in,
    second_out,
    gain_second,
):
    chip, core = lax.axis_index("dp"), lax.axis_index("shard")
    chips, cores = lax.axis_size("dp"), lax.axis_size("shard")
    routes = [
        Route(2, (0, 2, 1, 3), chips, cores),
        Route(3, (0, 1, 2, 3), chips, cores),
        Route(4, (0, 2), chips, cores),
        Route(5, (0, 1), chips, cores),
    ]
    meta = jnp.stack([core, lengths[0]] + [r.rank(chip, core) for r in routes]).astype(jnp.int32)
    line = Line()

    gains_own = low(gains).reshape(1, -1)
    gains_other = core_swap(gains_own)
    out_all = lax.all_gather(
        line(lambda v: cast_rows(v, 640), w_out), "shard", axis=0, tiled=True
    )
    gain_all = line(lambda a, b: wide(join_columns(a, b, core)), gains_own, gains_other)
    valid = lax.broadcasted_iota(jnp.int32, (SLOT_ROWS, 1), 0) < lengths[0]
    e = line(lambda v: jnp.where(valid, v, jnp.zeros((), BF)), cotangent)
    e_got = core_swap(e)
    qkv_own = line(cast_qkv, w_in)
    qkv_other = core_swap(qkv_own)
    mix_own = line(cast_mix, w_in)
    mix_other = [core_swap(rows) for rows in mix_own]
    cosine, sine = (jnp.asarray(table) for table in rope_constants())

    o, qkv, u, lse, a_own, a_other = line(
        forward,
        meta,
        tokens,
        gain_all,
        cosine,
        sine,
        qkv_own,
        qkv_other,
    )
    a_got = core_swap(a_other)
    o, e_got, a_got = lax.optimization_barrier((o, e_got, a_got))
    y, dgate, dup, b_own, b_other, left, send, dmid, dlow, small = line(
        unit, meta, o, tokens, e, gain_all, out_all, *mix_own, *mix_other
    )
    left_got, b_got = core_swap(send), core_swap(b_other)
    dgate_got, dup_got = core_swap(dgate), core_swap(dup)

    out, mix, qkv_sum = (
        Sum(line, routes[at], name) for at, name in zip(SUM_ROUTES, ("out", "mix", "qkv"))
    )
    states_in = (w_in, first_in, second_in)
    states_out = (w_out, first_out, second_out)
    now = {"in": (), "out": (), "small": small}
    back_inputs = (
        meta, dmid, dlow, tokens, gain_all, cosine, sine, out_all, qkv_own, qkv_other, qkv, u, lse, small,
    )

    def heads():
        now["dx"], *du, now["small"] = line(backward, *back_inputs)
        now["du"] = [(own, core_swap(own)) for own in du]

    def small_start():
        now["small_got"] = core_swap(now["small"])
        now["stage"] = 0

    def small_next():
        now["small"] = line(lambda a, b: a + b, now["small"], now["small_got"])
        if now["stage"] < 4:
            now["small_got"] = routes[1].swap(now["small"], now["stage"])
            now["stage"] += 1

    def begin_in(total, lefts, rights):
        spans = [(left, first, count) for left, _, _, first, count in rights]
        operands = [v for pair in lefts for v in pair] + [v for right in rights for v in right[1:3]]

        def operation(*o):
            pairs = list(zip(o[::2], o[1::2]))
            return grad_in(
                meta,
                pairs[: len(lefts)],
                [
                    (left, *pair, first, count)
                    for pair, (left, first, count) in zip(pairs[len(lefts) :], spans)
                ],
                total.route,
            )

        total.begin(operation, *operands)

    def begin_mix():
        begin_in(
            mix,
            [(b_own, b_got)],
            [(0, dgate, dgate_got, 1, 2), (0, dup, dup_got, 0, 3)],
        )

    def begin_qkv():
        begin_in(
            qkv_sum,
            [(a_own, a_got), (b_own, b_got)],
            [(0, own, got, 0, 1) for own, got in now["du"]] + [(1, dgate, dgate_got, 0, 1)],
        )

    def update(total, name, states, block, place, joint, part=None):
        gradients = (total.near if part != 1 else []) + (total.far if part != 0 else [])
        count = len(gradients)
        now[name] = line(
            lambda *o: adam_call(
                meta,
                total.route,
                o[:count],
                o[count : count + 3],
                o[count + 3 :],
                block,
                place,
                part or 0,
                joint,
            ),
            *gradients,
            *states,
            *now[name],
        )

    updates = {
        "mix": functools.partial(update, mix, "in", states_in, 1280, lambda j: 4 + j, True),
        "out": functools.partial(update, out, "out", states_out, 512, lambda j: j, False),
        "qkv": functools.partial(update, qkv_sum, "in", states_in, 1280, lambda j: j, True),
    }
    steps = {
        "mix": begin_mix,
        "out": lambda: out.begin(
            lambda *o: grad_out(meta, *o, out.route), left, left_got, dlow, e, e_got
        ),
        "qkv": begin_qkv,
        "K": heads,
        "small": small_start,
        "small+": small_next,
    }
    for name, total in (("mix", mix), ("out", out), ("qkv", qkv_sum)):
        steps[name + ">"] = total.add_sent
        steps[name + "*"] = total.add_kept
        steps[name + "+"] = total.add
        steps[name + "-"] = total.back
        steps[name + "="] = total.join
        steps[name + "!"] = updates[name]
        for part in range(2):
            steps[name + "!" + str(part)] = functools.partial(updates[name], part=part)
    for step in SCHEDULE:
        steps[step]()

    small = now["small"]
    valid_rms = jnp.sqrt(
        jnp.stack([small[3, 0], small[2, 512]]) / (small[4, 0] * MODEL_WIDTH)
    )
    gain_sum = lax.dynamic_slice_in_dim(
        jnp.concatenate([small[0], small[1], small[2, :256]]), core * gains.shape[0], gains.shape[0]
    )
    new_gains, new_gain_first, new_gain_second = adam(
        gains, gain_first, gain_second, gain_sum, GAIN_RATE, 0.0
    )
    return (
        y,
        now["dx"],
        now["in"][0],
        now["out"][0],
        new_gains,
        now["in"][1],
        now["out"][1],
        new_gain_first,
        now["in"][2],
        now["out"][2],
        new_gain_second,
        valid_rms,
    )


def solution(mesh):
    in_specs = (
        P(("dp", "shard"), None),
        P(("dp", "shard"), None),
        P(("dp", "shard")),
        P("shard", None),
        P("shard", None),
        P("shard"),
        P("shard", None),
        P("shard", None),
        P("shard"),
        P("shard", None),
        P("shard", None),
        P("shard"),
    )
    out_specs = (
        P(("dp", "shard"), None),
        P(("dp", "shard"), None),
        P("shard", None),
        P("shard", None),
        P("shard"),
        P("shard", None),
        P("shard", None),
        P("shard"),
        P("shard", None),
        P("shard", None),
        P("shard"),
        P(),
    )
    chips, cores = mesh.shape["dp"], mesh.shape["shard"]
    program = slot_shards if cores == 2 and chips == 16 else shards
    return jax.shard_map(program, mesh=mesh, in_specs=in_specs, out_specs=out_specs, check_vma=False)
```

```python
import functools
import math

import jax
import jax.numpy as jnp
import numpy as np
from jax import lax
from jax.experimental import pallas as pl
from jax.experimental.pallas import tpu as pltpu
from jax.sharding import PartitionSpec as P

MODEL_WIDTH = 1024
FF = 3072
QUERY_HEADS = 16
KEY_VALUE_HEADS = 8
HEAD_SIZE = 128
SLOT_ROWS = 512
STEP = 7
QKVC = 4096
GN = 2304


EPSILON = 1e-06
BETA_ONE = 0.9
BETA_TWO = 0.95
ADAM_EPSILON = 1e-08
MATRIX_RATE = 0.05
GAIN_RATE = 0.3
MATRIX_DECAY = 0.1
NEG_LARGE = -1e30


def rms_scale(values, gain):
    return values * lax.rsqrt(jnp.mean(values * values, axis=-1, keepdims=True) + EPSILON) * gain


def rope_tables(length, size):
    positions = jnp.arange(length, dtype=jnp.float32)
    half_index = jnp.arange(size // 2, dtype=jnp.float32)
    frequency = jnp.exp(half_index * (-2.0 * math.log(1000000.0) / size))
    angles = positions[:, None] * frequency[None, :]
    angles = jnp.concatenate([angles, angles], axis=1)
    return (jnp.cos(angles), jnp.sin(angles))


def rotate(values, cosine, sine):
    half_size = values.shape[-1] // 2
    turned = jnp.concatenate([-values[..., half_size:], values[..., :half_size]], axis=-1)
    return values * cosine[:, None, :] + turned * sine[:, None, :]


def prepare(unnormed_rows, gain_q, gain_k, cosine, sine):
    leading_rows = unnormed_rows.shape[:-1]
    queries = unnormed_rows[..., : QUERY_HEADS * HEAD_SIZE].reshape(
        leading_rows + (QUERY_HEADS, HEAD_SIZE)
    )
    key_head_rows = unnormed_rows[
        ..., QUERY_HEADS * HEAD_SIZE : (QUERY_HEADS + KEY_VALUE_HEADS) * HEAD_SIZE
    ].reshape(leading_rows + (KEY_VALUE_HEADS, HEAD_SIZE))
    value_head_rows = unnormed_rows[..., (QUERY_HEADS + KEY_VALUE_HEADS) * HEAD_SIZE :].reshape(
        leading_rows + (KEY_VALUE_HEADS, HEAD_SIZE)
    )
    queries = rotate(rms_scale(queries, gain_q), cosine, sine)
    key_head_rows = rotate(rms_scale(key_head_rows, gain_k), cosine, sine)
    return (queries, key_head_rows, value_head_rows)


def gated_unit(mixed):
    return jax.nn.silu(mixed[..., :FF]) * mixed[..., FF:]


def adamw_update(weight, first, second, gradient, rate, decay):
    first = BETA_ONE * first + (1.0 - BETA_ONE) * gradient
    second = BETA_TWO * second + (1.0 - BETA_TWO) * gradient * gradient
    corr_one = 1.0 - BETA_ONE**STEP
    corr_two = 1.0 - BETA_TWO**STEP
    update = first / corr_one / (jnp.sqrt(second / corr_two) + ADAM_EPSILON) + decay * weight
    return (weight - rate * update, first, second)


def outer_sum(left, right):
    return lax.dot_general(
        left, right, (((0,), (0,)), ((), ())), preferred_element_type=jnp.float32
    )


def back_product(gradient, weight):
    return lax.dot_general(
        gradient, weight, (((1,), (1,)), ((), ())), preferred_element_type=jnp.float32
    )


def key_mask(row_count, key_reach, length):
    query_pos = jnp.arange(row_count, dtype=jnp.int32)
    key_pos = jnp.arange(key_reach, dtype=jnp.int32)
    return (key_pos[None, :] <= query_pos[:, None]) & (key_pos[None, :] < length)


def slot_attention(query_low, key_low, value_low, length):
    block_rows = min(512, SLOT_ROWS)
    score_scale = HEAD_SIZE ** (-0.5)
    scores = (
        jnp.einsum("hgqd,hkd->hgqk", query_low, key_low, preferred_element_type=jnp.float32)
        * score_scale
    )
    scores = jnp.where(key_mask(block_rows, block_rows, length), scores, NEG_LARGE)
    row_peak = jnp.max(scores, axis=-1, keepdims=True)
    exp_values = jnp.exp(scores - row_peak)
    exp_total = jnp.sum(exp_values, axis=-1, keepdims=True)
    soft_weights = (exp_values / exp_total).astype(jnp.bfloat16)
    outputs = [
        jnp.einsum(
            "hgqk,hkd->hgqd", soft_weights, value_low, preferred_element_type=jnp.float32
        ).astype(jnp.bfloat16)
    ]
    totals = [row_peak + jnp.log(exp_total)]
    return (jnp.concatenate(outputs, axis=2), jnp.concatenate(totals, axis=2))


def slot_attention_back(query_low, key_low, value_low, totals, heads_gradient, length):
    block_rows = min(512, SLOT_ROWS)
    score_scale = HEAD_SIZE ** (-0.5)
    grad_keys = jnp.zeros(key_low.shape, jnp.float32)
    value_gradients = jnp.zeros(value_low.shape, jnp.float32)
    scores = (
        jnp.einsum("hgqd,hkd->hgqk", query_low, key_low, preferred_element_type=jnp.float32)
        * score_scale
    )
    allowed = key_mask(block_rows, block_rows, length)
    soft_weights = jnp.where(allowed, jnp.exp(scores - totals[:, :, 0:block_rows]), 0.0)
    back_soft = jnp.einsum(
        "hgqd,hkd->hgqk", heads_gradient, value_low, preferred_element_type=jnp.float32
    )
    inner_sums = jnp.sum(soft_weights * back_soft, axis=-1, keepdims=True)
    back_scores = (soft_weights * (back_soft - inner_sums)).astype(jnp.bfloat16)
    query_parts = [
        jnp.einsum("hgqk,hkd->hgqd", back_scores, key_low, preferred_element_type=jnp.float32)
        * score_scale
    ]
    grad_keys = grad_keys.at[:, :block_rows].add(
        jnp.einsum("hgqk,hgqd->hkd", back_scores, query_low, preferred_element_type=jnp.float32)
        * score_scale
    )
    value_gradients = value_gradients.at[:, :block_rows].add(
        jnp.einsum(
            "hgqk,hgqd->hkd",
            soft_weights.astype(jnp.bfloat16),
            heads_gradient,
            preferred_element_type=jnp.float32,
        )
    )
    return (jnp.concatenate(query_parts, axis=2), grad_keys, value_gradients)


def shards(
    tokens,
    cotangent,
    lengths,
    w_in,
    w_out,
    gains,
    first_in,
    first_out,
    gain_first,
    second_in,
    second_out,
    gain_second,
):
    slot_batch = lengths.shape[0]
    row_total = tokens.shape[0]
    query_group_width = QUERY_HEADS // KEY_VALUE_HEADS
    gathered_in, gathered_out, gathered_gains = (
        lax.all_gather(w_in.astype(jnp.bfloat16), "shard", axis=0, tiled=True),
        lax.all_gather(w_out.astype(jnp.bfloat16), "shard", axis=0, tiled=True),
        lax.all_gather(gains.astype(jnp.bfloat16), "shard", axis=0, tiled=True),
    )
    gain_all = gathered_gains.astype(jnp.float32)
    gain_in = gain_all[:MODEL_WIDTH]
    gain_post = gain_all[MODEL_WIDTH : 2 * MODEL_WIDTH]
    gain_query = gain_all[2 * MODEL_WIDTH : 2 * MODEL_WIDTH + HEAD_SIZE]
    gain_key = gain_all[2 * MODEL_WIDTH + HEAD_SIZE :]
    proj_qkv = gathered_in[:, :QKVC]
    proj_mix = gathered_in[:, QKVC:]
    proj_attn = gathered_out[: QUERY_HEADS * HEAD_SIZE]
    proj_down = gathered_out[QUERY_HEADS * HEAD_SIZE :]
    cosine, sine = rope_tables(SLOT_ROWS, HEAD_SIZE)
    layer_inputs = tokens.astype(jnp.float32)
    normed, pull_in = jax.vjp(rms_scale, layer_inputs, gain_in)
    normed_low = normed.astype(jnp.bfloat16)
    unnormed_rows = jnp.dot(normed_low, proj_qkv, preferred_element_type=jnp.float32).reshape(
        slot_batch, SLOT_ROWS, QKVC
    )

    def prep_local(raw_part, gain_q, gain_k):
        return prepare(raw_part, gain_q, gain_k, cosine, sine)

    (queries, key_head_rows, value_head_rows), pull_prep = jax.vjp(
        prep_local, unnormed_rows, gain_query, gain_key
    )
    query_low = (
        queries.astype(jnp.bfloat16)
        .reshape(slot_batch, SLOT_ROWS, KEY_VALUE_HEADS, query_group_width, HEAD_SIZE)
        .transpose(0, 2, 3, 1, 4)
    )
    key_low = key_head_rows.astype(jnp.bfloat16).transpose(0, 2, 1, 3)
    value_low = value_head_rows.astype(jnp.bfloat16).transpose(0, 2, 1, 3)
    attended, totals = lax.map(
        lambda slot_item: slot_attention(slot_item[0], slot_item[1], slot_item[2], slot_item[3]),
        (query_low, key_low, value_low, lengths),
    )
    attended_rows = attended.transpose(0, 3, 1, 2, 4).reshape(row_total, QUERY_HEADS * HEAD_SIZE)
    middle = layer_inputs + jnp.dot(attended_rows, proj_attn, preferred_element_type=jnp.float32)
    normed_post, pull_post = jax.vjp(rms_scale, middle, gain_post)
    post_low = normed_post.astype(jnp.bfloat16)
    mixed = jnp.dot(post_low, proj_mix, preferred_element_type=jnp.float32)
    hidden, pull_gate = jax.vjp(gated_unit, mixed)
    hidden_low = hidden.astype(jnp.bfloat16)
    layer_output = (
        middle + jnp.dot(hidden_low, proj_down, preferred_element_type=jnp.float32)
    ).astype(jnp.bfloat16)
    positions = jnp.arange(SLOT_ROWS, dtype=jnp.int32)
    valid_row_count = (
        (positions[None, :] < lengths[:, None]).astype(jnp.float32).reshape(row_total, 1)
    )
    back_out = cotangent.astype(jnp.float32) * valid_row_count
    back_out_low = back_out.astype(jnp.bfloat16)
    grad_down = outer_sum(hidden_low, back_out_low)
    back_hidden = back_product(back_out_low, proj_down)
    (back_mixed,) = pull_gate(back_hidden)
    mixed_low = back_mixed.astype(jnp.bfloat16)
    grad_mix = outer_sum(post_low, mixed_low)
    back_post = back_product(mixed_low, proj_mix)
    back_middle, grad_gain_post = pull_post(back_post)
    back_middle = back_middle + back_out
    middle_low = back_middle.astype(jnp.bfloat16)
    grad_attn = outer_sum(attended_rows, middle_low)
    attended_gradient = back_product(middle_low, proj_attn).astype(jnp.bfloat16)
    heads_gradient = attended_gradient.reshape(
        slot_batch, SLOT_ROWS, KEY_VALUE_HEADS, query_group_width, HEAD_SIZE
    ).transpose(0, 2, 3, 1, 4)
    grad_query, grad_key, grad_value = lax.map(
        lambda slot_item: slot_attention_back(
            slot_item[0], slot_item[1], slot_item[2], slot_item[3], slot_item[4], slot_item[5]
        ),
        (query_low, key_low, value_low, totals, heads_gradient, lengths),
    )
    grad_query = grad_query.transpose(0, 3, 1, 2, 4).reshape(
        slot_batch, SLOT_ROWS, QUERY_HEADS, HEAD_SIZE
    )
    grad_key = grad_key.transpose(0, 2, 1, 3)
    grad_value = grad_value.transpose(0, 2, 1, 3)
    back_raw, grad_gain_query, grad_gain_key = pull_prep((grad_query, grad_key, grad_value))
    raw_low = back_raw.reshape(row_total, QKVC).astype(jnp.bfloat16)
    grad_qkv = outer_sum(normed_low, raw_low)
    back_normed = back_product(raw_low, proj_qkv)
    back_inputs, grad_gain_in = pull_in(back_normed)
    layer_input_gradient = (back_middle + back_inputs).astype(jnp.bfloat16)
    output_values = layer_output.astype(jnp.float32)
    value_gradients = layer_input_gradient.astype(jnp.float32)
    sum_out, sum_grad, sum_count = lax.psum(
        (
            jnp.sum(valid_row_count * output_values * output_values),
            jnp.sum(valid_row_count * value_gradients * value_gradients),
            jnp.sum(valid_row_count),
        ),
        ("dp", "shard"),
    )
    valid_rms = jnp.sqrt(jnp.stack([sum_out, sum_grad]) / (sum_count * MODEL_WIDTH))
    owners = lax.axis_size("shard")
    grad_in = jnp.concatenate([grad_qkv, grad_mix], axis=1)
    grad_out = jnp.concatenate([grad_attn, grad_down], axis=0)
    grad_gain = jnp.concatenate(
        [grad_gain_in, grad_gain_post, grad_gain_query, grad_gain_key]
    ).reshape(owners, GN // owners)
    part_in, part_out, part_gain = (
        lax.psum_scatter(grad_in, "dp", scatter_dimension=1, tiled=True),
        lax.psum_scatter(grad_out, "dp", scatter_dimension=1, tiled=True),
        lax.psum_scatter(grad_gain, "dp", scatter_dimension=1, tiled=True),
    )
    owned_in, owned_out, owned_gain = (
        lax.psum_scatter(part_in, "shard", scatter_dimension=0, tiled=True),
        lax.psum_scatter(part_out, "shard", scatter_dimension=0, tiled=True),
        lax.psum_scatter(part_gain, "shard", scatter_dimension=0, tiled=True),
    )
    summed_in, summed_out, summed_gain = (
        lax.all_gather(owned_in, "dp", axis=1, tiled=True),
        lax.all_gather(owned_out, "dp", axis=1, tiled=True),
        lax.all_gather(owned_gain, "dp", axis=1, tiled=True),
    )
    summed_gain = summed_gain.reshape(-1)
    new_w_in, new_first_in, new_second_in = adamw_update(
        w_in, first_in, second_in, summed_in, MATRIX_RATE, MATRIX_DECAY
    )
    new_w_out, new_first_out, new_second_out = adamw_update(
        w_out, first_out, second_out, summed_out, MATRIX_RATE, MATRIX_DECAY
    )
    new_gains, new_gain_first, new_gain_second = adamw_update(
        gains, gain_first, gain_second, summed_gain, GAIN_RATE, 0.0
    )
    return (
        layer_output,
        layer_input_gradient,
        new_w_in,
        new_w_out,
        new_gains,
        new_first_in,
        new_first_out,
        new_gain_first,
        new_second_in,
        new_second_out,
        new_gain_second,
        valid_rms,
    )


def low(values):
    return values.astype(jnp.bfloat16)


def wide(values):
    return values.astype(jnp.float32)


def mul(left, right):
    return jnp.dot(left, right, preferred_element_type=jnp.float32)


def mul_bt(left, right):
    return lax.dot_general(
        left, right, (((1,), (1,)), ((), ())), preferred_element_type=jnp.float32
    )


def mul_at(left, right):
    return lax.dot_general(
        left, right, (((0,), (0,)), ((), ())), preferred_element_type=jnp.float32
    )


def whole(shape):
    return pl.BlockSpec(shape, lambda *_: (0,) * len(shape))


def resident(shape, index=None):
    index = index or (0,) * len(shape)
    return pl.BlockSpec(shape, lambda *_: index, pipeline_mode=pl.Buffered(1))


def shape_of(shape, kind):
    return jax.ShapeDtypeStruct(shape, kind)


GAIN_IN = slice(0, MODEL_WIDTH)
GAIN_POST = slice(MODEL_WIDTH, 2 * MODEL_WIDTH)
GAIN_Q = slice(2 * MODEL_WIDTH, 2 * MODEL_WIDTH + HEAD_SIZE)
GAIN_K = slice(2 * MODEL_WIDTH + HEAD_SIZE, GN)
BF = jnp.bfloat16
F32 = jnp.float32
VMEM_BYTES = 64 * 1024 * 1024


def params(axes=1, limit=VMEM_BYTES):
    return pltpu.CompilerParams(
        dimension_semantics=("arbitrary",) * axes, vmem_limit_bytes=limit
    )


def split_columns(values, core):
    half = values.shape[1] // 2
    first, second = values[:, :half], values[:, half:]
    mine = core == 0
    return jnp.where(mine, first, second), jnp.where(mine, second, first)


def join_columns(own, other, core):
    mine = core == 0
    return jnp.concatenate(
        [jnp.where(mine, own, other), jnp.where(mine, other, own)], axis=1
    )


def cast_qkv_kernel(q_ref, k_ref, v_ref, out_ref):
    for at in range(out_ref.shape[0]):
        out_ref[at, :, :256] = low(q_ref[:, at * 256 : at * 256 + 256])
        out_ref[at, :, 256:384] = low(k_ref[:, at * 128 : at * 128 + 128])
        out_ref[at, :, 384:] = low(v_ref[:, at * 128 : at * 128 + 128])


def cast_qkv(w_in):
    rows = w_in.shape[0]
    width = 256
    return pl.pallas_call(
        cast_qkv_kernel,
        grid=(KEY_VALUE_HEADS * 128 // width,),
        in_specs=[
            pl.BlockSpec((rows, 2 * width), lambda g: (0, g)),
            pl.BlockSpec((rows, width), lambda g: (0, 2048 // width + g)),
            pl.BlockSpec((rows, width), lambda g: (0, 3072 // width + g)),
        ],
        out_specs=pl.BlockSpec((width // 128, rows, 512), lambda g: (g, 0, 0)),
        out_shape=shape_of((KEY_VALUE_HEADS, rows, 512), BF),
        compiler_params=params(),
        name="cast_qkv",
    )(w_in, w_in, w_in)


def cast_rows_kernel(in_ref, out_ref):
    out_ref[...] = low(in_ref[...])


def cast_rows(values, block):
    rows, columns = values.shape
    spec = pl.BlockSpec((block, columns), lambda i: (i, 0))
    return pl.pallas_call(
        cast_rows_kernel,
        grid=(rows // block,),
        in_specs=[spec],
        out_specs=spec,
        out_shape=shape_of(values.shape, BF),
        compiler_params=params(),
        name="cast_out",
    )(values)


def cast_mix_kernel(gate_ref, up_ref, *out_refs):
    half = gate_ref.shape[0] // 2
    for at, out_ref in enumerate(out_refs):
        rows = slice(at * half, at * half + half)
        out_ref[0, :, :FFB] = low(gate_ref[rows, :])
        out_ref[0, :, FFB:] = low(up_ref[rows, :])


FFB = 1024
FF_STEPS = FF // FFB


def cast_mix(w_in):
    rows = w_in.shape[0]
    return pl.pallas_call(
        cast_mix_kernel,
        grid=(FF_STEPS,),
        in_specs=[
            pl.BlockSpec((rows, FFB), lambda j: (0, QKVC // FFB + j)),
            pl.BlockSpec((rows, FFB), lambda j: (0, (QKVC + FF) // FFB + j)),
        ],
        out_specs=[pl.BlockSpec((1, rows // 2, 2 * FFB), lambda j: (j, 0, 0))] * 2,
        out_shape=[shape_of((FF_STEPS, rows // 2, 2 * FFB), BF)] * 2,
        compiler_params=params(),
        name="cast_mix",
    )(w_in, w_in)


def turn(values):
    return pltpu.roll(values, HEAD_SIZE // 2, 1)


def head_norm(raw):
    scale = lax.rsqrt(jnp.mean(raw * raw, axis=-1, keepdims=True) + EPSILON)
    return raw * scale, scale


def block_mask(first_row, rows, keys, length):
    row = first_row + lax.broadcasted_iota(jnp.int32, (2 * rows, keys), 0) % rows
    key = lax.broadcasted_iota(jnp.int32, (2 * rows, keys), 1)
    return (key <= row) & (key < length)


def both_heads(values):
    return jnp.concatenate([values[:, :128], values[:, 128:]], axis=0)


QB = 128


def forward_kernel(
    meta_ref,
    x_ref,
    gain_ref,
    cos_ref,
    sin_ref,
    own_ref,
    other_ref,
    o_ref,
    qkv_ref,
    u_ref,
    lse_ref,
    a_own_ref,
    a_other_ref,
):
    core, length = meta_ref[0], meta_ref[1]

    @pl.when(pl.program_id(0) == 0)
    def _():
        x = wide(x_ref[...])
        scale = lax.rsqrt(jnp.mean(x * x, axis=-1, keepdims=True) + EPSILON)
        own, other = split_columns(low(x * scale * gain_ref[:, GAIN_IN]), core)
        a_own_ref[...] = own
        a_other_ref[...] = other

    u = mul(a_own_ref[...], own_ref[0]) + mul(a_other_ref[...], other_ref[0])
    u_ref[0] = u[:, :384]
    cosine, sine = cos_ref[...], sin_ref[...]
    gain_q, gain_k = gain_ref[:, GAIN_Q], gain_ref[:, GAIN_K]
    for part in range(3):
        normed, _ = head_norm(u[:, part * 128 : part * 128 + 128])
        normed = normed * (gain_k if part == 2 else gain_q)
        qkv_ref[0, :, part * 128 : part * 128 + 128] = low(
            normed * cosine + turn(normed) * sine
        )
    qkv_ref[0, :, 384:] = low(u[:, 384:])
    score_scale = HEAD_SIZE ** (-0.5)
    for first in range(0, SLOT_ROWS, QB):
        keys = first + QB
        rows = slice(first, first + QB)
        k = qkv_ref[0, :keys, 256:384]
        v = qkv_ref[0, :keys, 384:]
        scores = mul_bt(both_heads(qkv_ref[0, rows, :256]), k) * score_scale
        scores = jnp.where(block_mask(first, QB, keys, length), scores, NEG_LARGE)
        peak = jnp.max(scores, axis=-1, keepdims=True)
        powers = jnp.exp(scores - peak)
        total = jnp.sum(powers, axis=-1, keepdims=True)
        o = low(mul(low(powers * (1.0 / total)), v))
        level = peak + jnp.log(total)
        for head in range(2):
            half = slice(head * QB, head * QB + QB)
            columns = slice(head * 128, head * 128 + 128)
            o_ref[rows, columns] = o[half]
            lse_ref[0, rows, columns] = jnp.broadcast_to(level[half], (QB, 128))


def forward(meta, tokens, gains, cosine, sine, own, other):
    rows = SLOT_ROWS
    half = MODEL_WIDTH // 2
    return pl.pallas_call(
        forward_kernel,
        grid_spec=pltpu.PrefetchScalarGridSpec(
            num_scalar_prefetch=1,
            grid=(KEY_VALUE_HEADS,),
            in_specs=[
                resident((rows, MODEL_WIDTH)),
                resident((1, GN)),
                resident((rows, HEAD_SIZE)),
                resident((rows, HEAD_SIZE)),
                pl.BlockSpec((1, half, 512), lambda g, _: (g, 0, 0)),
                pl.BlockSpec((1, half, 512), lambda g, _: (g, 0, 0)),
            ],
            out_specs=[
                pl.BlockSpec((rows, 256), lambda g, _: (0, g)),
                pl.BlockSpec((1, rows, 512), lambda g, _: (g, 0, 0)),
                pl.BlockSpec((1, rows, 384), lambda g, _: (g, 0, 0)),
                pl.BlockSpec((1, rows, 256), lambda g, _: (g, 0, 0)),
                whole((rows, half)),
                whole((rows, half)),
            ],
        ),
        out_shape=[
            shape_of((rows, QUERY_HEADS * HEAD_SIZE), BF),
            shape_of((KEY_VALUE_HEADS, rows, 512), BF),
            shape_of((KEY_VALUE_HEADS, rows, 384), F32),
            shape_of((KEY_VALUE_HEADS, rows, 256), F32),
            shape_of((rows, half), BF),
            shape_of((rows, half), BF),
        ],
        compiler_params=params(),
        name="forward",
    )(meta, tokens, gains, cosine, sine, own, other)


def unit_kernel(
    meta_ref,
    o_ref,
    x_ref,
    e_ref,
    gain_ref,
    wo_ref,
    wd_ref,
    own_top_ref,
    own_end_ref,
    other_top_ref,
    other_end_ref,
    y_ref,
    dgate_ref,
    dup_ref,
    b_own_ref,
    b_other_ref,
    left_ref,
    send_ref,
    dmid_ref,
    dlow_ref,
    small_ref,
    mid_s,
    y_s,
    db_own_s,
    db_other_s,
):
    core, length = meta_ref[0], meta_ref[1]
    step = pl.program_id(0)
    quarter = own_top_ref.shape[1]
    weights = [
        (b_own_ref, slice(0, quarter), db_own_s, own_top_ref),
        (b_own_ref, slice(quarter, None), db_own_s, own_end_ref),
        (b_other_ref, slice(0, quarter), db_other_s, other_top_ref),
        (b_other_ref, slice(quarter, None), db_other_s, other_end_ref),
    ]
    attended = QUERY_HEADS * HEAD_SIZE
    valid = lax.broadcasted_iota(jnp.int32, (SLOT_ROWS, 1), 0) < length

    @pl.when(step == 0)
    def _():
        middle = wide(x_ref[...]) + mul(o_ref[...], wo_ref[...])
        mid_s[...] = middle
        y_s[...] = middle
        scale = lax.rsqrt(jnp.mean(middle * middle, axis=-1, keepdims=True) + EPSILON)
        own, other = split_columns(low(middle * scale * gain_ref[:, GAIN_POST]), core)
        b_own_ref[...] = own
        b_other_ref[...] = other
        db_own_s[...] = jnp.zeros_like(db_own_s)
        db_other_s[...] = jnp.zeros_like(db_other_s)

        @pl.when(core == 0)
        def _():
            left_ref[:, :attended] = o_ref[...]

        @pl.when(core != 0)
        def _():
            send_ref[:, :attended] = o_ref[...]

    e = e_ref[...]
    gate = sum(mul(b_ref[:, rows], w_ref[0, :, :FFB]) for b_ref, rows, _, w_ref in weights)
    up = sum(mul(b_ref[:, rows], w_ref[0, :, FFB:]) for b_ref, rows, _, w_ref in weights)
    down = wd_ref[...]
    dh = mul_bt(e, down)
    sigma = 1.0 / (1.0 + jnp.exp(-gate))
    silu = gate * sigma
    hidden = low(silu * up)
    dgate_ref[...] = low(dh * up * (sigma * (1.0 + gate * (1.0 - sigma))))
    dup_ref[...] = low(dh * silu)
    y_s[...] += mul(hidden, down)
    for _, rows, db_s, w_ref in weights:
        db_s[:, rows] += mul_bt(dgate_ref[...], w_ref[0, :, :FFB]) + mul_bt(
            dup_ref[...], w_ref[0, :, FFB:]
        )

    place = pl.multiple_of(jnp.maximum(step * FFB - 512, 0), 512)

    def place_hidden(first_ref, rest_ref):
        @pl.when(step == 0)
        def _():
            first_ref[:, attended : attended + 512] = hidden[:, :512]
            rest_ref[:, :512] = hidden[:, 512:]

        @pl.when(step != 0)
        def _():
            rest_ref[:, pl.ds(place, FFB)] = hidden

    @pl.when(core == 0)
    def _():
        place_hidden(left_ref, send_ref)

    @pl.when(core != 0)
    def _():
        place_hidden(send_ref, left_ref)

    @pl.when(step == FF_STEPS - 1)
    def _():
        y = low(y_s[...])
        y_ref[...] = y
        y = wide(y)
        total = jnp.sum(jnp.where(valid, y * y, 0.0))
        db = join_columns(db_own_s[...], db_other_s[...], core)
        middle = mid_s[...]
        scale = lax.rsqrt(jnp.mean(middle * middle, axis=-1, keepdims=True) + EPSILON)
        normed = middle * scale
        dn = db * gain_ref[:, GAIN_POST]
        dmid = wide(e) + scale * (
            dn - normed * jnp.mean(dn * normed, axis=-1, keepdims=True)
        )
        dmid_ref[...] = dmid
        dlow = low(dmid)
        dlow_ref[...] = dlow
        send_ref[:, left_ref.shape[1] :] = dlow
        small_ref[0:1, :] = jnp.sum(db * normed, axis=0, keepdims=True)
        small_ref[1:8, :] = jnp.full((7, MODEL_WIDTH), total)


def unit(meta, o, tokens, e, gains, w_out, *mix):
    rows = SLOT_ROWS
    half = MODEL_WIDTH // 2
    attended = QUERY_HEADS * HEAD_SIZE
    owned = w_out.shape[0] // 2
    return pl.pallas_call(
        unit_kernel,
        grid_spec=pltpu.PrefetchScalarGridSpec(
            num_scalar_prefetch=1,
            grid=(FF_STEPS,),
            in_specs=[
                resident((rows, attended)),
                resident((rows, MODEL_WIDTH)),
                resident((rows, MODEL_WIDTH)),
                resident((1, GN)),
                resident((attended, MODEL_WIDTH)),
                pl.BlockSpec((FFB, MODEL_WIDTH), lambda j, _: (attended // FFB + j, 0)),
            ]
            + [pl.BlockSpec((1, half // 2, 2 * FFB), lambda j, _: (j, 0, 0))] * 4,
            out_specs=[
                whole((rows, MODEL_WIDTH)),
                pl.BlockSpec((rows, FFB), lambda j, _: (0, j)),
                pl.BlockSpec((rows, FFB), lambda j, _: (0, j)),
                whole((rows, half)),
                whole((rows, half)),
                whole((rows, owned)),
                whole((rows, owned + MODEL_WIDTH)),
                whole((rows, MODEL_WIDTH)),
                whole((rows, MODEL_WIDTH)),
                whole((8, MODEL_WIDTH)),
            ],
            scratch_shapes=[
                pltpu.VMEM((rows, MODEL_WIDTH), F32),
                pltpu.VMEM((rows, MODEL_WIDTH), F32),
                pltpu.VMEM((rows, half), F32),
                pltpu.VMEM((rows, half), F32),
            ],
        ),
        out_shape=[
            shape_of((rows, MODEL_WIDTH), BF),
            shape_of((rows, FF), BF),
            shape_of((rows, FF), BF),
            shape_of((rows, half), BF),
            shape_of((rows, half), BF),
            shape_of((rows, owned), BF),
            shape_of((rows, owned + MODEL_WIDTH), BF),
            shape_of((rows, MODEL_WIDTH), F32),
            shape_of((rows, MODEL_WIDTH), BF),
            shape_of((8, MODEL_WIDTH), F32),
        ],
        compiler_params=params(),
        name="unit",
    )(meta, o, tokens, e, gains, w_out, w_out, *mix)


def backward_kernel(
    meta_ref,
    dmid_ref,
    dlow_ref,
    x_ref,
    gain_ref,
    cos_ref,
    sin_ref,
    wo_ref,
    own_ref,
    other_ref,
    qkv_ref,
    u_ref,
    lse_ref,
    small_in_ref,
    dx_ref,
    duq_first_ref,
    duq_last_ref,
    duk_ref,
    duv_ref,
    small_ref,
    da_own_s,
    da_other_s,
    head_s,
    dk_s,
    dv_s,
):
    core, length = meta_ref[0], meta_ref[1]
    step = pl.program_id(0)

    @pl.when(step == 0)
    def _():
        for sums in (da_own_s, da_other_s, head_s):
            sums[...] = jnp.zeros_like(sums)

    cosine, sine = cos_ref[...], sin_ref[...]
    score_scale = HEAD_SIZE ** (-0.5)
    do = low(mul_bt(dlow_ref[...], wo_ref[...]))

    def through(grad, raw, gain, slot):
        back = grad * cosine - turn(grad) * sine
        normed, scale = head_norm(raw)
        head_s[slot : slot + 1, :] += jnp.sum(back * normed, axis=0, keepdims=True)
        dn = back * gain
        return low(scale * (dn - normed * jnp.mean(dn * normed, axis=-1, keepdims=True)))

    grad_rows = []
    for first in reversed(range(0, SLOT_ROWS, QB)):
        keys = first + QB
        rows = slice(first, first + QB)
        q = both_heads(qkv_ref[0, rows, :256])
        k = qkv_ref[0, :keys, 256:384]
        v = qkv_ref[0, :keys, 384:]
        dos = both_heads(do[rows, :])
        level = jnp.concatenate([lse_ref[0, rows, 0:1], lse_ref[0, rows, 128:129]], axis=0)
        soft = jnp.where(
            block_mask(first, QB, keys, length),
            jnp.exp(mul_bt(q, k) * score_scale - level),
            0.0,
        )
        dsoft = mul_bt(dos, v)
        inner = jnp.sum(soft * dsoft, axis=-1, keepdims=True)
        ds = low(soft * (dsoft - inner))
        grad_rows.insert(0, mul(ds, k))
        grad_k = mul_at(ds, q)
        grad_v = mul_at(low(soft), dos)
        if keys == SLOT_ROWS:
            dk_s[...] = grad_k
            dv_s[...] = grad_v
        else:
            dk_s[:keys, :] += grad_k
            dv_s[:keys, :] += grad_v
    parts = []
    for head in range(2):
        columns = slice(head * 128, head * 128 + 128)
        grad_q = jnp.concatenate([g[head * QB : head * QB + QB] for g in grad_rows], axis=0)
        parts.append(
            through(grad_q * score_scale, u_ref[0, :, columns], gain_ref[:, GAIN_Q], 0)
        )
    parts.append(
        through(dk_s[...] * score_scale, u_ref[0, :, 256:384], gain_ref[:, GAIN_K], 1)
    )
    parts.append(low(dv_s[...]))
    du = jnp.concatenate(parts, axis=1)
    duk_ref[...] = du[:, 256:384]
    duv_ref[...] = du[:, 384:]

    @pl.when(step < KEY_VALUE_HEADS // 2)
    def _():
        duq_first_ref[...] = du[:, :256]

    @pl.when(step >= KEY_VALUE_HEADS // 2)
    def _():
        duq_last_ref[...] = du[:, :256]

    da_own_s[...] += mul_bt(du, own_ref[0])
    da_other_s[...] += mul_bt(du, other_ref[0])

    @pl.when(step == KEY_VALUE_HEADS - 1)
    def _():
        da = join_columns(da_own_s[...], da_other_s[...], core)
        x = wide(x_ref[...])
        scale = lax.rsqrt(jnp.mean(x * x, axis=-1, keepdims=True) + EPSILON)
        normed = x * scale
        dn = da * gain_ref[:, GAIN_IN]
        dx = low(
            dmid_ref[...]
            + scale * (dn - normed * jnp.mean(dn * normed, axis=-1, keepdims=True))
        )
        dx_ref[...] = dx
        dx = wide(dx)
        valid = lax.broadcasted_iota(jnp.int32, (SLOT_ROWS, 1), 0) < length
        total = jnp.sum(jnp.where(valid, dx * dx, 0.0))
        small_ref[0:1, :] = jnp.sum(da * normed, axis=0, keepdims=True)
        small_ref[1:2, :] = small_in_ref[0:1, :]
        small_ref[2:8, :] = jnp.full((6, MODEL_WIDTH), total)
        small_ref[2:3, 0:128] = head_s[0:1, :]
        small_ref[2:3, 128:256] = head_s[1:2, :]
        small_ref[3:4, :] = small_in_ref[1:2, :]
        small_ref[4:5, :] = jnp.full((1, MODEL_WIDTH), 1.0) * length.astype(F32)


def backward(
    meta,
    dmid,
    dlow,
    tokens,
    gains,
    cosine,
    sine,
    w_out,
    own,
    other,
    qkv,
    u,
    lse,
    small,
):
    rows = SLOT_ROWS
    half = MODEL_WIDTH // 2
    middle = KEY_VALUE_HEADS // 2
    return pl.pallas_call(
        backward_kernel,
        grid_spec=pltpu.PrefetchScalarGridSpec(
            num_scalar_prefetch=1,
            grid=(KEY_VALUE_HEADS,),
            in_specs=[
                resident((rows, MODEL_WIDTH)),
                resident((rows, MODEL_WIDTH)),
                resident((rows, MODEL_WIDTH)),
                resident((1, GN)),
                resident((rows, HEAD_SIZE)),
                resident((rows, HEAD_SIZE)),
                pl.BlockSpec((256, MODEL_WIDTH), lambda g, _: (g, 0)),
                pl.BlockSpec((1, half, 512), lambda g, _: (g, 0, 0)),
                pl.BlockSpec((1, half, 512), lambda g, _: (g, 0, 0)),
                pl.BlockSpec((1, rows, 512), lambda g, _: (g, 0, 0)),
                pl.BlockSpec((1, rows, 384), lambda g, _: (g, 0, 0)),
                pl.BlockSpec((1, rows, 256), lambda g, _: (g, 0, 0)),
                resident((8, MODEL_WIDTH)),
            ],
            out_specs=[
                whole((rows, MODEL_WIDTH)),
                pl.BlockSpec((rows, 256), lambda g, _: (0, jnp.minimum(g, middle - 1))),
                pl.BlockSpec((rows, 256), lambda g, _: (0, jnp.maximum(g - middle, 0))),
                pl.BlockSpec((rows, 128), lambda g, _: (0, g)),
                pl.BlockSpec((rows, 128), lambda g, _: (0, g)),
                whole((8, MODEL_WIDTH)),
            ],
            scratch_shapes=[
                pltpu.VMEM((rows, half), F32),
                pltpu.VMEM((rows, half), F32),
                pltpu.VMEM((8, HEAD_SIZE), F32),
                pltpu.VMEM((rows, HEAD_SIZE), F32),
                pltpu.VMEM((rows, HEAD_SIZE), F32),
            ],
        ),
        out_shape=[shape_of((rows, MODEL_WIDTH), BF)]
        + [shape_of((rows, 1024), BF)] * 4
        + [shape_of((8, MODEL_WIDTH), F32)],
        compiler_params=params(),
        name="backward",
    )(meta, dmid, dlow, tokens, gains, cosine, sine, w_out, own, other, qkv, u, lse, small)


def store_pieces(acc, rank, pieces, targets):
    piece = acc.shape[0] // pieces
    share = pieces // len(targets)
    for at in range(pieces):
        source = pl.multiple_of(lax.bitwise_xor(at, rank) * piece, piece)
        place = at % share
        targets[at // share][place * piece : (place + 1) * piece, :] = low(
            acc[pl.ds(source, piece), :]
        )


def quarters(rows, columns):
    return [shape_of((rows // 4, columns), BF)] * 4


def grad_in_kernel(meta_ref, *refs, route, lefts, spans):
    sources, (*targets, acc) = refs[: 2 * (lefts + len(spans))], refs[2 * (lefts + len(spans)) :]
    step = pl.program_id(0)
    for at, (left, start, stop, _) in enumerate(spans):
        l_own, l_got = sources[2 * left : 2 * left + 2]
        r_own, r_got = sources[2 * (lefts + at) : 2 * (lefts + at) + 2]

        @pl.when((step >= start) & (step < stop))
        def _():
            acc[...] = mul_at(l_own[...], r_own[...]) + mul_at(l_got[...], r_got[...])

    store_pieces(acc, meta_ref[route.slot], route.pieces, targets)


def grad_in(meta, lefts, rights, route, block=1024):
    tokens, rows = lefts[0][0].shape
    spans, count = [], 0
    for left, _, _, first, blocks in rights:
        spans.append((left, count, count + blocks, first))
        count += blocks
    outs = quarters(rows, count * block)
    out = pl.BlockSpec((outs[0].shape[0], block), lambda j, _: (0, j))

    def right_spec(start, stop, first):
        return pl.BlockSpec(
            (tokens, block), lambda j, _: (0, first + jnp.clip(j, start, stop - 1) - start)
        )

    return pl.pallas_call(
        functools.partial(grad_in_kernel, route=route, lefts=len(lefts), spans=spans),
        grid_spec=pltpu.PrefetchScalarGridSpec(
            num_scalar_prefetch=1,
            grid=(count,),
            in_specs=[resident((tokens, rows))] * (2 * len(lefts))
            + [right_spec(*span[1:]) for span in spans for _ in range(2)],
            out_specs=[out] * len(outs),
            scratch_shapes=[pltpu.VMEM((rows, block), F32)],
        ),
        out_shape=outs,
        compiler_params=params(),
        name="grad_in",
    )(meta, *(v for left in lefts for v in left), *(v for right in rights for v in right[1:3]))


def grad_out_kernel(
    meta_ref, l_own, l_got, d_own, d_got, e_own, e_got, *targets, route
):
    *targets, acc = targets
    attended = QUERY_HEADS * HEAD_SIZE
    acc[attended:, :] = mul_at(l_own[:, attended:], e_own[...]) + mul_at(
        l_got[:, attended:], e_got[...]
    )

    def upper(own, got):
        for at in range(0, attended, 512):
            rows = slice(at, at + 512)
            acc[rows, :] = mul_at(l_own[:, rows], own) + mul_at(l_got[:, rows], got)

    @pl.when(meta_ref[0] == 0)
    def _():
        upper(d_own[...], d_got[...])

    @pl.when(meta_ref[0] != 0)
    def _():
        upper(e_own[...], e_got[...])

    store_pieces(acc, meta_ref[route.slot], route.pieces, targets)


def grad_out(meta, l_own, got, d_own, e_own, e_got, route):
    tokens, rows = l_own.shape
    block = 512
    outs = quarters(rows, MODEL_WIDTH)
    left = resident((tokens, rows))
    right = pl.BlockSpec((tokens, block), lambda j, _: (0, j))
    out = pl.BlockSpec((outs[0].shape[0], block), lambda j, _: (0, j))
    return pl.pallas_call(
        functools.partial(grad_out_kernel, route=route),
        grid_spec=pltpu.PrefetchScalarGridSpec(
            num_scalar_prefetch=1,
            grid=(MODEL_WIDTH // block,),
            in_specs=[
                left,
                left,
                right,
                pl.BlockSpec((tokens, block), lambda j, _: (0, rows // block + j)),
                right,
                right,
            ],
            out_specs=[out] * len(outs),
            scratch_shapes=[pltpu.VMEM((rows, block), F32)],
        ),
        out_shape=outs,
        compiler_params=params(),
        name="grad_out",
    )(meta, l_own, got, d_own, got, e_own, e_got)


class Route:
    def __init__(self, slot, bits, chips, cores):
        self.slot, self.chips, self.cores = slot, chips, cores
        even = list(bits)
        crossed = {0: 1, 1: 0}
        self.orders = [even, [crossed.get(bit, bit) for bit in even]]
        self.stages = len(even)
        self.pieces = 1 << self.stages
        self.groups = {}
        for chip in range(chips):
            for core in range(cores):
                kept = sum(1 << bit for bit in self.orders[core % 2])
                self.groups.setdefault((core, chip & kept), []).append(chip * cores + core)
        self.groups = list(self.groups.values())
        self.whole = len(self.groups) == chips * cores

    def rank(self, chip, core):
        def code(order):
            value = 0
            for bit in order:
                value = 2 * value + ((chip >> bit) & 1)
            return value

        return jnp.where(core % 2 == 0, code(self.orders[0]), code(self.orders[1]))

    def swap(self, values, stage):
        pairs = [
            (
                chip * self.cores + core,
                (chip ^ (1 << self.orders[core % 2][stage])) * self.cores + core,
            )
            for chip in range(self.chips)
            for core in range(self.cores)
        ]
        return lax.ppermute(values, ("dp", "shard"), pairs)


class Line:
    def __init__(self):
        self.last = None

    def __call__(self, operation, *operands):
        if self.last is not None:
            operands = lax.optimization_barrier((*operands, self.last))[:-1]
        result = operation(*operands)
        self.last = result[0] if isinstance(result, (tuple, list)) else result
        return result


class Sum:
    def __init__(self, line, route, name):
        self.line, self.route, self.name = line, route, name

    def swap(self, values, stage, what):
        with jax.named_scope(f"{self.name}_{what}_{stage}"):
            return self.route.swap(values, stage)

    def begin(self, operation, *operands):
        *self.keeps, send, first = self.line(operation, *operands)
        self.first_got = self.swap(first, 0, "halving_first")
        self.got = self.swap(send, 0, "halving")
        self.stage = 0

    def add_sent(self):
        send = self.line(lambda a, b: low(wide(a) + wide(b)), self.keeps[1], self.first_got)
        self.next_got = self.swap(send, 1, "halving")

    def add_kept(self):
        self.keep = self.line(lambda a, b: low(wide(a) + wide(b)), self.keeps[0], self.got)
        self.got, self.stage = self.next_got, 1

    def add(self):
        half = self.keep.shape[0] // 2
        if self.stage == self.route.stages - 1:
            self.mine = self.line(lambda a, b: low(wide(a) + wide(b)), self.keep, self.got)
            if self.route.whole:
                self.got = self.swap(self.mine, self.stage, "doubling")
            else:
                with jax.named_scope(f"{self.name}_rest"):
                    self.mine = lax.psum(
                        self.mine, ("dp", "shard"), axis_index_groups=self.route.groups
                    )
            return
        send = self.line(lambda a, b: low(wide(a[half:]) + wide(b[half:])), self.keep, self.got)
        self.stage += 1
        got = self.swap(send, self.stage, "halving")
        self.keep = self.line(lambda a, b: low(wide(a[:half]) + wide(b[:half])), self.keep, self.got)
        self.got = got

    def back(self):
        self.mine = lax.optimization_barrier((self.mine, self.line.last))[0]
        self.got = self.swap(self.mine, 1, "doubling")
        self.far = [self.swap(self.mine, 0, "doubling")]

    def join(self):
        if self.stage > 1:
            self.mine = self.line(
                lambda a, b: jnp.concatenate([a, b], axis=0), self.mine, self.got
            )
            self.stage -= 1
            self.got = self.swap(self.mine, self.stage, "doubling")
            if self.stage == 1:
                self.far = [self.swap(self.mine, 0, "doubling")]
        else:
            self.got = lax.optimization_barrier((self.got, self.line.last))[0]
            self.far.append(self.swap(self.got, 0, "doubling_last"))
            self.near = [self.mine, self.got]


def adam(weight, first, second, gradient, rate, decay):
    first = BETA_ONE * first + (1.0 - BETA_ONE) * gradient
    second = BETA_TWO * second + ((1.0 - BETA_TWO) * gradient) * gradient
    square = second * (1.0 / (1.0 - BETA_TWO**STEP))
    root = square * lax.rsqrt(square) + ADAM_EPSILON
    step = (first * (rate / (1.0 - BETA_ONE**STEP))) / root
    return weight * (1.0 - rate * decay) - step, first, second


def adam_kernel(meta_ref, *refs, route, joint, parts):
    pairs = [refs[2 * at : 2 * at + 2] for at in range(parts)]
    w_ref, f_ref, s_ref = refs[2 * parts : 2 * parts + 3]
    new_w, new_f, new_s = refs[-3:]
    pieces = route.pieces // 2 if joint else route.pieces // 4
    piece = w_ref.shape[0] // pieces
    inner = lax.rem(meta_ref[route.slot], pieces)
    share = route.pieces // 4

    def update(*g_refs):
        for at in range(pieces):
            source = pl.multiple_of(lax.bitwise_xor(at, inner) % share * piece, piece)
            there = slice(at * piece, (at + 1) * piece)
            new_w[there, :], new_f[there, :], new_s[there, :] = adam(
                w_ref[there, :],
                f_ref[there, :],
                s_ref[there, :],
                wide(g_refs[at // share][pl.ds(source, piece), :]),
                MATRIX_RATE,
                MATRIX_DECAY,
            )

    step = pl.program_id(0)
    for at, (near, far) in enumerate(pairs):
        now = (step if joint else step // 2) == at
        near_first = inner < share if joint else step % 2 == 0

        @pl.when(now & near_first)
        def _():
            update(near, far)

        @pl.when(now & jnp.logical_not(near_first))
        def _():
            update(far, near)


def adam_call(meta, route, gradients, states, done, block, place, part, joint):
    rows, columns = gradients[0].shape
    parts = len(gradients) // 2
    steps = 1 if joint else 2
    tall = rows * 2 // steps
    last = columns // block - 1

    def g_spec(at):
        first = at // 2 if joint else at
        return pl.BlockSpec(
            (rows, block),
            lambda t, j, m: (0, jnp.where(t == first, j, jnp.where(t < first, 0, last))),
        )

    spec = pl.BlockSpec(
        (tall, block),
        lambda t, j, m: (
            lax.bitwise_xor(t + part * steps, m[route.slot] // (route.pieces // (2 * steps))),
            place(j),
        ),
    )
    return pl.pallas_call(
        functools.partial(adam_kernel, route=route, joint=joint, parts=parts),
        grid_spec=pltpu.PrefetchScalarGridSpec(
            num_scalar_prefetch=1,
            grid=(parts * steps, columns // block),
            in_specs=[g_spec(at) for at in range(2 * parts)]
            + [spec, spec, spec]
            + [pl.BlockSpec(memory_space=pl.ANY)] * len(done),
            out_specs=[spec, spec, spec],
        ),
        out_shape=[shape_of(states[0].shape, F32)] * 3,
        input_output_aliases={4 + 2 * parts + i: i for i in range(len(done))},
        compiler_params=params(2),
        name="adam",
    )(meta, *gradients, *states, *done)


def rope_constants():
    index = np.arange(HEAD_SIZE // 2, dtype=np.float32)
    frequency = np.exp(index * np.float32(-2.0 * math.log(1000000.0) / HEAD_SIZE))
    angles = np.arange(SLOT_ROWS, dtype=np.float32)[:, None] * frequency[None, :]
    cosine, sine = np.cos(angles), np.sin(angles)
    return (
        np.concatenate([cosine, cosine], axis=1).astype(np.float32),
        np.concatenate([-sine, sine], axis=1).astype(np.float32),
    )


def core_swap(values):
    return lax.ppermute(values, "shard", [(0, 1), (1, 0)])


SUM_ROUTES = (0, 1, 3)

SCHEDULE = (
    "out", "mix", "out>", "K", "small", "mix>", "out*", "mix*", "out+", "mix+", "qkv",
    "out+", "mix+", "qkv>", "mix+", "out+", "mix=", "qkv*", "out=", "small+", "qkv+",
    "small+", "mix=", "out=", "small+", "mix=", "mix!0", "small+", "out=", "out!0", "qkv-",
    "mix!1", "out!1", "qkv=", "qkv!0", "small+", "qkv!1",
)


def slot_shards(
    tokens,
    cotangent,
    lengths,
    w_in,
    w_out,
    gains,
    first_in,
    first_out,
    gain_first,
    second_in,
    second_out,
    gain_second,
):
    chip, core = lax.axis_index("dp"), lax.axis_index("shard")
    chips, cores = lax.axis_size("dp"), lax.axis_size("shard")
    routes = [
        Route(2, (0, 2, 1, 3), chips, cores),
        Route(3, (0, 1, 2, 3), chips, cores),
        Route(4, (0, 2), chips, cores),
        Route(5, (0, 1), chips, cores),
    ]
    meta = jnp.stack([core, lengths[0]] + [r.rank(chip, core) for r in routes]).astype(jnp.int32)
    line = Line()

    gains_own = low(gains).reshape(1, -1)
    gains_other = core_swap(gains_own)
    out_all = lax.all_gather(
        line(lambda v: cast_rows(v, 640), w_out), "shard", axis=0, tiled=True
    )
    gain_all = line(lambda a, b: wide(join_columns(a, b, core)), gains_own, gains_other)
    valid = lax.broadcasted_iota(jnp.int32, (SLOT_ROWS, 1), 0) < lengths[0]
    e = line(lambda v: jnp.where(valid, v, jnp.zeros((), BF)), cotangent)
    e_got = core_swap(e)
    qkv_own = line(cast_qkv, w_in)
    qkv_other = core_swap(qkv_own)
    mix_own = line(cast_mix, w_in)
    mix_other = [core_swap(rows) for rows in mix_own]
    cosine, sine = (jnp.asarray(table) for table in rope_constants())

    o, qkv, u, lse, a_own, a_other = line(
        forward,
        meta,
        tokens,
        gain_all,
        cosine,
        sine,
        qkv_own,
        qkv_other,
    )
    a_got = core_swap(a_other)
    o, e_got, a_got = lax.optimization_barrier((o, e_got, a_got))
    y, dgate, dup, b_own, b_other, left, send, dmid, dlow, small = line(
        unit, meta, o, tokens, e, gain_all, out_all, *mix_own, *mix_other
    )
    left_got, b_got = core_swap(send), core_swap(b_other)
    dgate_got, dup_got = core_swap(dgate), core_swap(dup)

    out, mix, qkv_sum = (
        Sum(line, routes[at], name) for at, name in zip(SUM_ROUTES, ("out", "mix", "qkv"))
    )
    states_in = (w_in, first_in, second_in)
    states_out = (w_out, first_out, second_out)
    now = {"in": (), "out": (), "small": small}
    back_inputs = (
        meta, dmid, dlow, tokens, gain_all, cosine, sine, out_all, qkv_own, qkv_other, qkv, u, lse, small,
    )

    def heads():
        now["dx"], *du, now["small"] = line(backward, *back_inputs)
        now["du"] = [(own, core_swap(own)) for own in du]

    def small_start():
        now["small_got"] = core_swap(now["small"])
        now["stage"] = 0

    def small_next():
        now["small"] = line(lambda a, b: a + b, now["small"], now["small_got"])
        if now["stage"] < 4:
            now["small_got"] = routes[1].swap(now["small"], now["stage"])
            now["stage"] += 1

    def begin_in(total, lefts, rights):
        spans = [(left, first, count) for left, _, _, first, count in rights]
        operands = [v for pair in lefts for v in pair] + [v for right in rights for v in right[1:3]]

        def operation(*o):
            pairs = list(zip(o[::2], o[1::2]))
            return grad_in(
                meta,
                pairs[: len(lefts)],
                [
                    (left, *pair, first, count)
                    for pair, (left, first, count) in zip(pairs[len(lefts) :], spans)
                ],
                total.route,
            )

        total.begin(operation, *operands)

    def begin_mix():
        begin_in(
            mix,
            [(b_own, b_got)],
            [(0, dgate, dgate_got, 1, 2), (0, dup, dup_got, 0, 3)],
        )

    def begin_qkv():
        begin_in(
            qkv_sum,
            [(a_own, a_got), (b_own, b_got)],
            [(0, own, got, 0, 1) for own, got in now["du"]] + [(1, dgate, dgate_got, 0, 1)],
        )

    def update(total, name, states, block, place, joint, part=None):
        gradients = (total.near if part != 1 else []) + (total.far if part != 0 else [])
        count = len(gradients)
        now[name] = line(
            lambda *o: adam_call(
                meta,
                total.route,
                o[:count],
                o[count : count + 3],
                o[count + 3 :],
                block,
                place,
                part or 0,
                joint,
            ),
            *gradients,
            *states,
            *now[name],
        )

    updates = {
        "mix": functools.partial(update, mix, "in", states_in, 1280, lambda j: 4 + j, True),
        "out": functools.partial(update, out, "out", states_out, 512, lambda j: j, False),
        "qkv": functools.partial(update, qkv_sum, "in", states_in, 1280, lambda j: j, True),
    }
    steps = {
        "mix": begin_mix,
        "out": lambda: out.begin(
            lambda *o: grad_out(meta, *o, out.route), left, left_got, dlow, e, e_got
        ),
        "qkv": begin_qkv,
        "K": heads,
        "small": small_start,
        "small+": small_next,
    }
    for name, total in (("mix", mix), ("out", out), ("qkv", qkv_sum)):
        steps[name + ">"] = total.add_sent
        steps[name + "*"] = total.add_kept
        steps[name + "+"] = total.add
        steps[name + "-"] = total.back
        steps[name + "="] = total.join
        steps[name + "!"] = updates[name]
        for part in range(2):
            steps[name + "!" + str(part)] = functools.partial(updates[name], part=part)
    for step in SCHEDULE:
        steps[step]()

    small = now["small"]
    valid_rms = jnp.sqrt(
        jnp.stack([small[3, 0], small[2, 512]]) / (small[4, 0] * MODEL_WIDTH)
    )
    gain_sum = lax.dynamic_slice_in_dim(
        jnp.concatenate([small[0], small[1], small[2, :256]]), core * gains.shape[0], gains.shape[0]
    )
    new_gains, new_gain_first, new_gain_second = adam(
        gains, gain_first, gain_second, gain_sum, GAIN_RATE, 0.0
    )
    return (
        y,
        now["dx"],
        now["in"][0],
        now["out"][0],
        new_gains,
        now["in"][1],
        now["out"][1],
        new_gain_first,
        now["in"][2],
        now["out"][2],
        new_gain_second,
        valid_rms,
    )


def solution(mesh):
    in_specs = (
        P(("dp", "shard"), None),
        P(("dp", "shard"), None),
        P(("dp", "shard")),
        P("shard", None),
        P("shard", None),
        P("shard"),
        P("shard", None),
        P("shard", None),
        P("shard"),
        P("shard", None),
        P("shard", None),
        P("shard"),
    )
    out_specs = (
        P(("dp", "shard"), None),
        P(("dp", "shard"), None),
        P("shard", None),
        P("shard", None),
        P("shard"),
        P("shard", None),
        P("shard", None),
        P("shard"),
        P("shard", None),
        P("shard", None),
        P("shard"),
        P(),
    )
    chips, cores = mesh.shape["dp"], mesh.shape["shard"]
    program = slot_shards if cores == 2 and chips == 16 else shards
    return jax.shard_map(program, mesh=mesh, in_specs=in_specs, out_specs=out_specs, check_vma=False)
```
